32 devices in a mesh: section: 4 (over x, core), dp: 8 (over z, y).
Axes of the slice: x: 2, y: 2, z: 4, core: 2. Of those that a mesh axis runs over, the one named last changes fastest.
Arguments:
- h_forward: bfloat16 [4, 8, 128, 3584], P('section', 'dp'), may hold values from -6 to 6
- h_reverse: bfloat16 [4, 8, 128, 3584], P('section', 'dp'), may hold values from -6 to 6
- weights: bfloat16 [4, 3584, 256], P('section', 'dp'), may hold values from -0.09375 to 0.09375
- gains: bfloat16 [4, 256], P('section'), may hold values from 0.25 to 1.75
Outputs:
- grad_forward: bfloat16 [4, 8, 128, 3584], P('section', 'dp')
- grad_reverse: bfloat16 [4, 8, 128, 3584], P('section', 'dp')
- grad_weights: float32 [4, 3584, 256], P('section', 'dp')
- grad_gains: float32 [4, 256], P('section')
The draws below stay inside these ranges and needn't reach their ends.
All inputs are finite; a program needn't handle non-finite values.
Results may differ from the reference program's by a relative error of at most 0.01.
Values may be sent and summed in bfloat16 or wider, within the bound.
No kernel may reach another device: no remote copies, remote signals or barrier semaphores. Data moves between devices by JAX's collectives and lax.ppermute only.
A program may use at most 64 MiB of HBM per device.

```python
import jax
import jax.numpy as jnp
from jax import lax

D = 3584
C = 256
TOK = 128
SECTIONS = 4
SEQS = 8


def shard_levels(stream_key, shape, shards, low, high):
    def one(axis_at, blocks):
        draws = jax.random.uniform(jax.random.fold_in(jax.random.fold_in(stream_key, 6), axis_at), (blocks,), jnp.float32, low / len(shards), high / len(shards))
        return jnp.repeat(jnp.exp(draws), shape[axis_at] // blocks).reshape((-1,) + (1,) * (len(shape) - axis_at - 1))

    level = one(*shards[0])
    for cut in shards[1:]:
        level = level * one(*cut)
    return level


def noise(rng, extent, deviation, limit, shards=(), kind=jnp.bfloat16):
    array = jax.random.normal(rng, extent, jnp.float32) * deviation
    if len(shards) > 0:
        array = shard_levels(rng, extent, shards, -0.22, 0.18) * array
    return jnp.clip(array, min=-limit, max=limit).astype(kind)


def setup_inputs(seed: int = 0) -> dict:
    streams_of = jax.random.split(jax.random.key(seed), 5)
    return {
        "h_forward": noise(streams_of[0], (SECTIONS, SEQS, TOK, D), 1.0, 6.0, ((0, 4), (1, 8))),
        "h_reverse": noise(streams_of[1], (SECTIONS, SEQS, TOK, D), 1.0, 6.0, ((0, 4), (1, 8))),
        "weights": noise(streams_of[2], (SECTIONS, D, C), D ** -0.5, 0.09375, ((0, 4), (1, 8))),
        "gains": jnp.clip(1.0 + 0.15 * jax.random.normal(streams_of[3], (SECTIONS, C), jnp.float32), 0.25, 1.75).astype(jnp.bfloat16),
    }


EPS = 1e-06

def group_forward(x, w, g):
    c = jnp.dot(x, w, preferred_element_type=jnp.float32)
    inv = lax.rsqrt(lax.optimization_barrier(jnp.mean(c * c, axis=-1, keepdims=True)) + EPS)
    normed = (c * inv * g.astype(jnp.float32)).astype(jnp.bfloat16)
    scale = 3.0 / c.shape[-1]
    scores = jnp.dot(normed, normed.T, preferred_element_type=jnp.float32) * scale
    count = x.shape[0]
    rows = lax.broadcasted_iota(jnp.int32, (count, count), 0)
    cols = lax.broadcasted_iota(jnp.int32, (count, count), 1)
    scores = jnp.where(cols <= rows, scores, -1e+30)
    top = lax.optimization_barrier(jnp.max(scores, axis=-1, keepdims=True))
    expo = jnp.exp(scores - top)
    probs = expo / lax.optimization_barrier(jnp.sum(expo, axis=-1, keepdims=True))
    probs_b = probs.astype(jnp.bfloat16)
    mixed = jnp.dot(probs_b, x, preferred_element_type=jnp.float32)
    out = (x.astype(jnp.float32) + mixed).astype(jnp.bfloat16)
    return (out, (c, inv, normed, probs, probs_b))

def group_backward(x, w, g, saved, grad_out):
    c, inv, normed, probs, probs_b = saved
    scale = 3.0 / c.shape[-1]
    dx = grad_out.astype(jnp.float32) + jnp.dot(probs_b.T, grad_out, preferred_element_type=jnp.float32)
    dprobs = jnp.dot(grad_out, x.T, preferred_element_type=jnp.float32)
    dscores = probs * (dprobs - lax.optimization_barrier(jnp.sum(dprobs * probs, axis=-1, keepdims=True)))
    dscores_b = (dscores * scale).astype(jnp.bfloat16)
    dnormed = jnp.dot(dscores_b, normed, preferred_element_type=jnp.float32) + jnp.dot(dscores_b.T, normed, preferred_element_type=jnp.float32)
    dgain = lax.optimization_barrier(jnp.sum(dnormed * c * inv, axis=0))
    dhat = dnormed * g.astype(jnp.float32)
    dc = inv * dhat - c * (inv * inv * inv) * lax.optimization_barrier(jnp.mean(dhat * c, axis=-1, keepdims=True))
    dc_b = dc.astype(jnp.bfloat16)
    dx = dx + jnp.dot(dc_b, w.T, preferred_element_type=jnp.float32)
    dw = jnp.dot(x.T, dc_b, preferred_element_type=jnp.float32)
    return (dx, dw, dgain)

def forward_all(hidden, wmats, gvecs):

    def section_fn(item):
        return jax.vmap(lambda x: group_forward(x, item[1], item[2])[0])(item[0])
    return lax.map(section_fn, (hidden, wmats, gvecs))

def second_back(inputs, wmats, gvecs):

    def seq_fn(x, w, g):
        y, saved = group_forward(x, w, g)
        return group_backward(x, w, g, saved, y)[0].astype(jnp.bfloat16)

    def section_fn(item):
        return jax.vmap(lambda x: seq_fn(x, item[1], item[2]))(item[0])
    return lax.map(section_fn, (inputs, wmats, gvecs))

def full_back(first_in, cotangent, second_in, wmats, gvecs):

    def seq_fn(x1, cot, x2, w, g):
        y2, saved2 = group_forward(x2, w, g)
        unused, dw2, dg2 = group_backward(x2, w, g, saved2, y2)
        y1, saved1 = group_forward(x1, w, g)
        dx1, dw1, dg1 = group_backward(x1, w, g, saved1, cot)
        part = lax.optimization_barrier((dw1 + dw2).astype(jnp.bfloat16)).astype(jnp.float32)
        return (dx1.astype(jnp.bfloat16), part, dg1 + dg2)

    def section_fn(item):
        dx, parts, dgs = jax.vmap(lambda a, b, e: seq_fn(a, b, e, item[3], item[4]))(item[0], item[1], item[2])
        return (dx, lax.optimization_barrier(jnp.sum(parts, axis=0)), lax.optimization_barrier(jnp.sum(dgs, axis=0)))
    return lax.map(section_fn, (first_in, cotangent, second_in, wmats, gvecs))

def reference(h_forward, h_reverse, weights, gains):
    twin_w = weights[::-1]
    twin_g = gains[::-1]
    u_f = forward_all(h_forward, weights, gains)
    a_f = jnp.roll(u_f, 1, axis=0)
    e_f = second_back(a_f, weights, gains)
    grad_forward, gw_f, gg_f = full_back(h_forward, jnp.roll(e_f, -1, axis=0), a_f, weights, gains)
    u_r = forward_all(h_reverse, twin_w, twin_g)
    a_r = jnp.roll(u_r, -1, axis=0)
    e_r = second_back(a_r, twin_w, twin_g)
    grad_reverse, gw_r, gg_r = full_back(h_reverse, jnp.roll(e_r, 1, axis=0), a_r, twin_w, twin_g)
    grad_weights = gw_f + gw_r[::-1]
    grad_gains = gg_f + gg_r[::-1]
    return (grad_forward, grad_reverse, grad_weights, grad_gains)
```

```python
import functools

import jax
import jax.numpy as jnp
from jax import lax
from jax.experimental import pallas as pl
from jax.experimental.pallas import tpu as pltpu
from jax.sharding import PartitionSpec as P

EPS = 1e-06
AXES = ("section", "dp")
BF16 = jnp.bfloat16
F32 = jnp.float32
CHUNK = 512
VMEM_LIMIT = 40 * 1024 * 1024


def matmul(a, b):
    return jnp.dot(a, b, preferred_element_type=F32)


def matmul_nt(a, b):
    return lax.dot_general(a, b, (((1,), (1,)), ((), ())), preferred_element_type=F32)


def matmul_tn(a, b):
    return lax.dot_general(a, b, (((0,), (0,)), ((), ())), preferred_element_type=F32)


def latent_norm(c, g):
    inv = lax.rsqrt(jnp.mean(c * c, axis=-1, keepdims=True) + EPS)
    return inv, (c * inv * g.astype(F32)).astype(BF16)


def attention(normed, width):
    scores = matmul_nt(normed, normed) * (3.0 / width)
    rows = lax.broadcasted_iota(jnp.int32, scores.shape, 0)
    cols = lax.broadcasted_iota(jnp.int32, scores.shape, 1)
    scores = jnp.where(cols <= rows, scores, -1e30)
    expo = jnp.exp(scores - jnp.max(scores, axis=-1, keepdims=True))
    return expo / jnp.sum(expo, axis=-1, keepdims=True)


def column_chunks(width):
    return [slice(at, at + CHUNK) for at in range(0, width, CHUNK)]


def mix_into(out_ref, x_ref, probs_b):
    for cols in column_chunks(x_ref.shape[-1]):
        x = x_ref[:, cols]
        out_ref[:, cols] = (x.astype(F32) + matmul(probs_b, x)).astype(BF16)


def score_grad(dy_ref, x_ref):
    total = None
    for cols in column_chunks(x_ref.shape[-1]):
        part = matmul_nt(dy_ref[:, cols], x_ref[:, cols])
        total = part if total is None else total + part
    return total


def latent_grad(dprobs, probs, c, inv, normed, g):
    scale = 3.0 / c.shape[-1]
    dscores = probs * (dprobs - jnp.sum(dprobs * probs, axis=-1, keepdims=True))
    dscores_b = (dscores * scale).astype(BF16)
    dnormed = matmul(dscores_b, normed) + matmul_tn(dscores_b, normed)
    dgain = jnp.sum(dnormed * c * inv, axis=0, keepdims=True)
    dhat = dnormed * g.astype(F32)
    dc = inv * dhat - c * (inv * inv * inv) * jnp.mean(dhat * c, axis=-1, keepdims=True)
    return dc.astype(BF16), dgain


def input_grad(out_ref, dy_ref, probs_b, dc_b, w_ref):
    for cols in column_chunks(dy_ref.shape[-1]):
        dy = dy_ref[:, cols]
        dx = dy.astype(F32) + matmul_tn(probs_b, dy) + matmul_nt(dc_b, w_ref[cols, :])
        out_ref[:, cols] = dx.astype(BF16)


def ring_place(value):
    return value ^ (value >> 1)


def shard_row(dy, steps, rows):
    dp = lax.axis_index("dp")
    place = (ring_place(dp >> 1) + steps) & 3
    return pl.multiple_of((ring_place(place) * 2 + ((dp & 1) ^ dy)) * rows, 16)


def copies(pairs, sems):
    return [pltpu.make_async_copy(a, b, sems.at[i]) for i, (a, b) in enumerate(pairs)]


def first_kernel(*refs):
    pieces, (gain_ref, hf_ref, hr_ref, u_ref, w_ref, c_ref, p_ref, sems) = refs[:16], refs[16:]
    rows = pieces[0].shape[0]
    pairs = []
    for dx in range(2):
        for dy in range(2):
            for k in range(4):
                at = shard_row(dy, 4 - k, rows)
                pairs.append((pieces[len(pairs)], w_ref.at[dx, pl.ds(at, rows), :]))
    moves = copies(pairs, sems)
    for move in moves:
        move.start()
    odd = lax.axis_index("section") & 1
    for slot, x_ref in enumerate((hf_ref, hr_ref)):
        for move in moves[8 * slot : 8 * slot + 8]:
            move.wait()
        g = gain_ref[slot : slot + 1, :]
        c = matmul(x_ref[...], w_ref[slot])
        _, normed = latent_norm(c, g)
        probs = attention(normed, c.shape[-1])
        c_ref[slot] = c
        p_ref[slot] = probs
        mix_into(u_ref.at[slot ^ odd], x_ref, probs.astype(BF16))


def second_kernel(gain_ref, x_ref, w_ref, e_ref, dc_ref, dg_ref, v_ref):
    even = 1 - (lax.axis_index("section") & 1)
    for slot in range(2):
        g = gain_ref[slot : slot + 1, :]
        x = x_ref.at[slot]
        c = matmul(x[...], w_ref[slot])
        inv, normed = latent_norm(c, g)
        probs = attention(normed, c.shape[-1])
        probs_b = probs.astype(BF16)
        mix_into(v_ref, x, probs_b)
        dc_b, dgain = latent_grad(score_grad(v_ref, x), probs, c, inv, normed, g)
        dc_ref[slot] = dc_b
        dg_ref[slot : slot + 1, :] = dgain
        input_grad(e_ref.at[slot ^ even], v_ref, probs_b, dc_b, w_ref.at[slot])


def third_kernel(*refs):
    ins, outs = refs[:11], refs[11:]
    gain_ref, hf_ref, hr_ref, w_ref, c_ref, p_ref, cot_ref, x2_ref, dc2_ref, dg2_ref, _ = ins
    gf_ref, gr_ref, dg_ref = outs[:3]
    pieces, (dw_ref, sems) = outs[3:19], outs[19:]
    rows = pieces[0].shape[0]
    pairs = []
    for dx in range(2):
        for dy in range(2):
            for k in range(4):
                at = shard_row(dy, k, rows)
                pairs.append((dw_ref.at[dx, pl.ds(at, rows), :], pieces[len(pairs)]))
    moves = copies(pairs, sems)
    for slot, x_ref, out_ref in ((1, hr_ref, gr_ref), (0, hf_ref, gf_ref)):
        g = gain_ref[slot : slot + 1, :]
        c = c_ref[slot]
        probs = p_ref[slot]
        inv, normed = latent_norm(c, g)
        cot = cot_ref.at[slot]
        dc_b, dgain = latent_grad(score_grad(cot, x_ref), probs, c, inv, normed, g)
        dg_ref[slot : slot + 1, :] = dgain + dg2_ref[slot : slot + 1, :]
        for cols in column_chunks(x_ref.shape[-1]):
            dw = matmul_tn(x_ref[:, cols], dc_b) + matmul_tn(x2_ref[slot, :, cols], dc2_ref[slot])
            dw_ref[slot, cols, :] = dw.astype(BF16)
        for move in moves[8 * slot : 8 * slot + 8]:
            move.start()
        input_grad(out_ref, cot, probs.astype(BF16), dc_b, w_ref.at[slot])
    for move in moves:
        move.wait()


def kernel_call(body, n_any, n_vmem, outs, out_any, scratch, flops):
    anywhere, local = pl.BlockSpec(memory_space=pl.ANY), pl.BlockSpec(memory_space=pltpu.VMEM)
    return pl.pallas_call(
        body,
        out_shape=outs,
        in_specs=[anywhere] * n_any + [local] * n_vmem,
        out_specs=[local] * (len(outs) - out_any) + [anywhere] * out_any,
        scratch_shapes=scratch,
        compiler_params=pltpu.CompilerParams(vmem_limit_bytes=VMEM_LIMIT),
        cost_estimate=pl.CostEstimate(flops=flops, bytes_accessed=8 << 20, transcendentals=0),
    )


def moves_between():
    def pairs(change):
        found = []
        for i in range(32):
            s, d = divmod(i, 8)
            to_s, to_d = change(s, d)
            found.append((i, to_s * 8 + to_d))
        return found

    following = {0: 1, 1: 3, 3: 2, 2: 0}
    changes = (
        lambda s, d: (s ^ 1, d),
        lambda s, d: (s ^ 2, d),
        lambda s, d: (s, d ^ 1),
        lambda s, d: (s, following[d >> 1] * 2 + (d & 1)),
        lambda s, d: (s, d ^ 2),
        lambda s, d: (s, d ^ 4),
    )
    return [functools.partial(lambda v, p: lax.ppermute(v, AXES, p), p=pairs(c)) for c in changes]


def after(value, *others):
    return lax.optimization_barrier((value, *others))[0]


def gather(shard, over_x, over_y, along_z):
    own, x, y, xy = [shard] + [None] * 3, [None] * 4, [None] * 4, [None] * 4
    x[0], y[0], own[1] = over_x(own[0]), over_y(own[0]), along_z(own[0])
    own[1] = after(own[1], x[0], y[0])
    xy[0], y[1], own[2] = over_x(y[0]), over_y(own[1]), along_z(own[1])
    x[1], y[2], own[3] = over_x(own[1]), over_y(own[2]), along_z(own[2])
    own[3] = after(own[3], xy[0], y[1])
    x[3], y[3], xy[1] = over_x(own[3]), over_y(own[3]), along_z(xy[0])
    x[2] = over_x(after(own[2], x[1]))
    xy[3], xy[2] = over_y(x[3]), along_z(xy[1])
    return own + y + x + xy


def add(*values):
    return sum(v.astype(F32) for v in values)


def scatter(parts, over_x, over_y, along_z):
    own, y, x, xy = parts[:4], parts[4:8], parts[8:12], parts[12:]

    def total(*values):
        return add(*values).astype(BF16)

    e1 = total(xy[1], along_z(xy[2]))
    c3 = total(x[3], over_y(xy[3]))
    s3 = total(own[3], over_x(c3), over_y(y[3]))
    e0 = total(xy[0], along_z(e1))
    s2 = total(own[2], over_x(x[2]), over_y(y[2]), along_z(s3))
    b0 = total(y[0], over_x(e0))
    s1 = total(own[1], over_x(x[1]), over_y(y[1]), along_z(s2))
    return add(own[0], over_x(x[0]), over_y(b0), along_z(s1))


def on_chip_relay(h_forward, h_reverse, weights, gains):
    other_core, over_x, over_y, along_z, z_near, z_far = moves_between()
    tokens, width = h_forward.shape[2:]
    rows, latent = weights.shape[1:]
    shard, gain = weights[0], gains
    x_fwd, x_rev = h_forward[0, 0], other_core(h_reverse[0, 0])
    both_gains = jnp.concatenate([gain, over_x(gain)], axis=0)
    shards = gather(shard, over_x, over_y, along_z)
    pair = jax.ShapeDtypeStruct((2, tokens, width), BF16)
    whole = jax.ShapeDtypeStruct((2, width, latent), BF16)
    saved_c = jax.ShapeDtypeStruct((2, tokens, latent), F32)
    saved_p = jax.ShapeDtypeStruct((2, tokens, tokens), F32)
    dgains = jax.ShapeDtypeStruct((2, latent), F32)
    dcs = jax.ShapeDtypeStruct((2, tokens, latent), BF16)
    one = jax.ShapeDtypeStruct((tokens, width), BF16)
    product = 2 * tokens * width * latent
    u, w, c1, p1 = kernel_call(
        first_kernel, 16, 3, [pair, whole, saved_c, saved_p], 0,
        [pltpu.SemaphoreType.DMA((16,))], 3 * product,
    )(*shards, both_gains, x_fwd, x_rev)
    x2 = other_core(u)
    e, dc2, dg2 = kernel_call(
        second_kernel, 0, 3, [pair, dcs, dgains], 0,
        [pltpu.VMEM((tokens, width), BF16)], 7 * product,
    )(both_gains, x2, w)
    cot = other_core(e)
    piece = jax.ShapeDtypeStruct((rows, latent), BF16)
    out = kernel_call(
        third_kernel, 0, 11, [one, one, dgains] + [piece] * 16, 16,
        [pltpu.VMEM((2, width, latent), BF16), pltpu.SemaphoreType.DMA((16,))], 8 * product,
    )(both_gains, x_fwd, x_rev, w, c1, p1, cot, x2, dc2, dg2, both_gains)
    grad_fwd, grad_rev, dgain = out[:3]
    grad_rev = other_core(grad_rev)
    grad_weights = scatter(out[3:], over_x, over_y, along_z)
    dgain = dgain[:1] + over_x(dgain[1:])
    dgain = dgain + over_y(dgain)
    dgain = dgain + z_near(dgain)
    dgain = dgain + z_far(dgain)
    return grad_fwd[None, None], grad_rev[None, None], grad_weights[None], dgain


def from_partner(value, axis, apart):
    mask = 2**apart
    pairs = [(source, source ^ mask) for source in range(lax.axis_size(axis))]
    return lax.ppermute(value, axis, pairs)


def passed_along(value, axis, by):
    devices = lax.axis_size(axis)
    return lax.ppermute(value, axis, [(i, (i + by) % devices) for i in range(devices)])


def group_forward(x, w, g):
    c = jnp.dot(x, w, preferred_element_type=jnp.float32)
    inv = lax.rsqrt(jnp.mean(c * c, axis=-1, keepdims=True) + EPS)
    normed = (c * inv * g.astype(jnp.float32)).astype(jnp.bfloat16)
    scale = 3.0 / c.shape[-1]
    scores = jnp.dot(normed, normed.T, preferred_element_type=jnp.float32) * scale
    count = x.shape[0]
    rows = lax.broadcasted_iota(jnp.int32, (count, count), 0)
    cols = lax.broadcasted_iota(jnp.int32, (count, count), 1)
    scores = jnp.where(cols <= rows, scores, -1e30)
    top = jnp.max(scores, axis=-1, keepdims=True)
    expo = jnp.exp(scores - top)
    probs = expo / jnp.sum(expo, axis=-1, keepdims=True)
    probs_b = probs.astype(jnp.bfloat16)
    mixed = jnp.dot(probs_b, x, preferred_element_type=jnp.float32)
    out = (x.astype(jnp.float32) + mixed).astype(jnp.bfloat16)
    return (out, (c, inv, normed, probs, probs_b))


def group_backward(x, w, g, saved, grad_out):
    c, inv, normed, probs, probs_b = saved
    scale = 3.0 / c.shape[-1]
    dx = grad_out.astype(jnp.float32) + jnp.dot(
        probs_b.T, grad_out, preferred_element_type=jnp.float32
    )
    dprobs = jnp.dot(grad_out, x.T, preferred_element_type=jnp.float32)
    dscores = probs * (dprobs - jnp.sum(dprobs * probs, axis=-1, keepdims=True))
    dscores_b = (dscores * scale).astype(jnp.bfloat16)
    dnormed = jnp.dot(dscores_b, normed, preferred_element_type=jnp.float32) + jnp.dot(
        dscores_b.T, normed, preferred_element_type=jnp.float32
    )
    dgain = jnp.sum(dnormed * c * inv, axis=0)
    dhat = dnormed * g.astype(jnp.float32)
    dc = inv * dhat - c * (inv * inv * inv) * jnp.mean(dhat * c, axis=-1, keepdims=True)
    dc_b = dc.astype(jnp.bfloat16)
    dx = dx + jnp.dot(dc_b, w.T, preferred_element_type=jnp.float32)
    dw = jnp.dot(x.T, dc_b, preferred_element_type=jnp.float32)
    return (dx, dw, dgain)


def twin_copy(pair):
    for bit in range(lax.axis_size("section").bit_length() - 1):
        pair = from_partner((pair[0], pair[1]), "section", bit)
    return (pair[0], pair[1])


def grad_twin(pair):
    for bit in range(lax.axis_size("section").bit_length() - 1):
        pair = (
            from_partner(pair[0].astype(jnp.bfloat16), "section", bit).astype(jnp.float32),
            from_partner(pair[1].astype(jnp.bfloat16), "section", bit).astype(jnp.float32),
        )
    return (pair[0], pair[1])


def neighbour(values, offset):
    return passed_along(values, "section", offset)


def sections_apart(h_forward, h_reverse, weights, gains):
    shard = weights[0]
    gain = gains[0]
    twin_shard, twin_gain = twin_copy((shard, gain))
    own, twin = (
        lax.all_gather(shard, "dp", axis=0, tiled=True),
        lax.all_gather(twin_shard, "dp", axis=0, tiled=True),
    )
    x_fwd = h_forward[0, 0]
    x_rev = h_reverse[0, 0]
    u_fwd, saved_f1 = group_forward(x_fwd, own, gain)
    u_rev, saved_r1 = group_forward(x_rev, twin, twin_gain)
    in_fwd = neighbour(u_fwd, 1)
    in_rev = neighbour(u_rev, -1)
    v_fwd, saved_f2 = group_forward(in_fwd, own, gain)
    v_rev, saved_r2 = group_forward(in_rev, twin, twin_gain)
    din_fwd, dw_f2, dg_f2 = group_backward(in_fwd, own, gain, saved_f2, v_fwd)
    din_rev, dw_r2, dg_r2 = group_backward(in_rev, twin, twin_gain, saved_r2, v_rev)
    back_fwd = neighbour(din_fwd.astype(jnp.bfloat16), -1)
    back_rev = neighbour(din_rev.astype(jnp.bfloat16), 1)
    dh_fwd, dw_f1, dg_f1 = group_backward(x_fwd, own, gain, saved_f1, back_fwd)
    dh_rev, dw_r1, dg_r1 = group_backward(x_rev, twin, twin_gain, saved_r1, back_rev)
    share_fwd, share_rev = (
        lax.psum_scatter(
            (dw_f1 + dw_f2).astype(jnp.bfloat16), "dp", scatter_dimension=0, tiled=True
        ).astype(jnp.float32),
        lax.psum_scatter(
            (dw_r1 + dw_r2).astype(jnp.bfloat16), "dp", scatter_dimension=0, tiled=True
        ).astype(jnp.float32),
    )
    gsum_fwd, gsum_rev = lax.psum((dg_f1 + dg_f2, dg_r1 + dg_r2), "dp")
    mirror_w, mirror_g = grad_twin((share_rev, gsum_rev))
    grad_weights = (share_fwd + mirror_w)[None]
    grad_gains = (gsum_fwd + mirror_g)[None]
    return (
        dh_fwd.astype(jnp.bfloat16)[None, None],
        dh_rev.astype(jnp.bfloat16)[None, None],
        grad_weights,
        grad_gains,
    )


def solution(mesh):
    in_specs = (
        P("section", "dp", None, None),
        P("section", "dp", None, None),
        P("section", "dp", None),
        P("section", None),
    )
    out_specs = (
        P("section", "dp", None, None),
        P("section", "dp", None, None),
        P("section", "dp", None),
        P("section", None),
    )
    on_chip = (mesh.shape["section"], mesh.shape["dp"]) == (4, 8)
    on_device = on_chip_relay if on_chip else sections_apart
    return jax.shard_map(
        on_device, mesh=mesh, in_specs=in_specs, out_specs=out_specs, check_vma=False
    )
```

```python
import functools

import jax
import jax.numpy as jnp
from jax import lax
from jax.experimental import pallas as pl
from jax.experimental.pallas import tpu as pltpu
from jax.sharding import PartitionSpec as P

EPS = 1e-06
AXES = ("section", "dp")
BF16 = jnp.bfloat16
F32 = jnp.float32
CHUNK = 512
VMEM_LIMIT = 40 * 1024 * 1024


def matmul(a, b):
    return jnp.dot(a, b, preferred_element_type=F32)


def matmul_nt(a, b):
    return lax.dot_general(a, b, (((1,), (1,)), ((), ())), preferred_element_type=F32)


def matmul_tn(a, b):
    return lax.dot_general(a, b, (((0,), (0,)), ((), ())), preferred_element_type=F32)


def latent_norm(c, g):
    inv = lax.rsqrt(jnp.mean(c * c, axis=-1, keepdims=True) + EPS)
    return inv, (c * inv * g.astype(F32)).astype(BF16)


def attention(normed, width):
    scores = matmul_nt(normed, normed) * (3.0 / width)
    rows = lax.broadcasted_iota(jnp.int32, scores.shape, 0)
    cols = lax.broadcasted_iota(jnp.int32, scores.shape, 1)
    scores = jnp.where(cols <= rows, scores, -1e30)
    expo = jnp.exp(scores - jnp.max(scores, axis=-1, keepdims=True))
    return expo / jnp.sum(expo, axis=-1, keepdims=True)


def column_chunks(width):
    return [slice(at, at + CHUNK) for at in range(0, width, CHUNK)]


def mix_into(out_ref, x_ref, probs_b):
    for cols in column_chunks(x_ref.shape[-1]):
        x = x_ref[:, cols]
        out_ref[:, cols] = (x.astype(F32) + matmul(probs_b, x)).astype(BF16)


def score_grad(dy_ref, x_ref):
    total = None
    for cols in column_chunks(x_ref.shape[-1]):
        part = matmul_nt(dy_ref[:, cols], x_ref[:, cols])
        total = part if total is None else total + part
    return total


def latent_grad(dprobs, probs, c, inv, normed, g):
    scale = 3.0 / c.shape[-1]
    dscores = probs * (dprobs - jnp.sum(dprobs * probs, axis=-1, keepdims=True))
    dscores_b = (dscores * scale).astype(BF16)
    dnormed = matmul(dscores_b, normed) + matmul_tn(dscores_b, normed)
    dgain = jnp.sum(dnormed * c * inv, axis=0, keepdims=True)
    dhat = dnormed * g.astype(F32)
    dc = inv * dhat - c * (inv * inv * inv) * jnp.mean(dhat * c, axis=-1, keepdims=True)
    return dc.astype(BF16), dgain


def input_grad(out_ref, dy_ref, probs_b, dc_b, w_ref):
    for cols in column_chunks(dy_ref.shape[-1]):
        dy = dy_ref[:, cols]
        dx = dy.astype(F32) + matmul_tn(probs_b, dy) + matmul_nt(dc_b, w_ref[cols, :])
        out_ref[:, cols] = dx.astype(BF16)


def ring_place(value):
    return value ^ (value >> 1)


def shard_row(dy, steps, rows):
    dp = lax.axis_index("dp")
    place = (ring_place(dp >> 1) + steps) & 3
    return pl.multiple_of((ring_place(place) * 2 + ((dp & 1) ^ dy)) * rows, 16)


def slot_of(chain):
    return chain ^ 1 ^ (lax.axis_index("section") & 1)


def first_block(slot, *refs):
    pieces, (gain_ref, x_ref, u_ref, w_ref, c_ref, p_ref) = refs[:8], refs[8:]
    rows = pieces[0].shape[0]
    for at, piece in enumerate(pieces):
        w_ref[pl.ds(shard_row(at // 4, 4 - at % 4, rows), rows), :] = piece[...]
    c = matmul(x_ref[...], w_ref[...])
    _, normed = latent_norm(c, gain_ref[slot : slot + 1, :])
    probs = attention(normed, c.shape[-1])
    c_ref[...] = c
    p_ref[...] = probs
    mix_into(u_ref, x_ref, probs.astype(BF16))


def second_block(chain, gain_ref, x_ref, w0_ref, w1_ref, e_ref, dc_ref, dg_ref, v_ref, c_ref):
    slot = slot_of(chain)
    g = jnp.where(slot == 0, gain_ref[0:1, :].astype(F32), gain_ref[1:2, :].astype(F32))
    for at, w_ref in enumerate((w0_ref, w1_ref)):

        @pl.when(slot == at)
        def _(w_ref=w_ref):
            c_ref[...] = matmul(x_ref[...], w_ref[...])

    c = c_ref[...]
    inv, normed = latent_norm(c, g)
    probs = attention(normed, c.shape[-1])
    probs_b = probs.astype(BF16)
    mix_into(v_ref, x_ref, probs_b)
    dc_b, dgain = latent_grad(score_grad(v_ref, x_ref), probs, c, inv, normed, g)
    dc_ref[...] = dc_b
    dg_ref[...] = dgain
    for at, w_ref in enumerate((w0_ref, w1_ref)):

        @pl.when(slot == at)
        def _(w_ref=w_ref):
            input_grad(e_ref, v_ref, probs_b, dc_b, w_ref)


def first_weight_grad(slot, *refs):
    gain_ref, x_ref, c_ref, p_ref, cot_ref, x2a_ref, x2b_ref, dc2a_ref, dc2b_ref, dg2a_ref, dg2b_ref = refs[:11]
    dc_ref, dg_ref = refs[11:13]
    pieces, (dw_ref, dcs_ref) = refs[13:21], refs[21:]
    tokens, rows = x_ref.shape[0], pieces[0].shape[0]
    g = gain_ref[slot : slot + 1, :]
    c, probs = c_ref[...], p_ref[...]
    inv, normed = latent_norm(c, g)
    dc_b, dgain = latent_grad(score_grad(cot_ref, x_ref), probs, c, inv, normed, g)
    dc_ref[...] = dc_b
    dcs_ref[:tokens, :] = dc_b
    for chain, x2_ref, dc2_ref, dg2_ref in ((0, x2a_ref, dc2a_ref, dg2a_ref), (1, x2b_ref, dc2b_ref, dg2b_ref)):

        @pl.when(slot_of(chain) == slot)
        def _(x2_ref=x2_ref, dc2_ref=dc2_ref, dg2_ref=dg2_ref):
            dg_ref[...] = dgain + dg2_ref[...]
            dcs_ref[tokens:, :] = dc2_ref[...]
            for cols in column_chunks(x_ref.shape[-1]):
                x = jnp.concatenate([x_ref[:, cols], x2_ref[:, cols]], axis=0)
                dw_ref[cols, :] = matmul_tn(x, dcs_ref[...]).astype(BF16)

    for at, piece in enumerate(pieces):
        piece[...] = dw_ref[pl.ds(shard_row(at // 4, at % 4, rows), rows), :]


def first_input_grad(cot_ref, p_ref, dc_ref, w_ref, out_ref):
    input_grad(out_ref, cot_ref, p_ref[...].astype(BF16), dc_ref[...], w_ref)


def kernel_call(body, args, outs, scratch=(), flops=0):
    local = pl.BlockSpec(memory_space=pltpu.VMEM)
    return pl.pallas_call(
        body,
        out_shape=outs,
        in_specs=[local] * len(args),
        out_specs=[local] * len(outs),
        scratch_shapes=scratch,
        compiler_params=pltpu.CompilerParams(vmem_limit_bytes=VMEM_LIMIT),
        cost_estimate=pl.CostEstimate(flops=flops, bytes_accessed=4 << 20, transcendentals=0),
    )(*args)


def moves_between():
    def pairs(change):
        found = []
        for i in range(32):
            s, d = divmod(i, 8)
            to_s, to_d = change(s, d)
            found.append((i, to_s * 8 + to_d))
        return found

    following = {0: 1, 1: 3, 3: 2, 2: 0}
    changes = (
        lambda s, d: (s ^ 1, d),
        lambda s, d: (s ^ 2, d),
        lambda s, d: (s, d ^ 1),
        lambda s, d: (s, following[d >> 1] * 2 + (d & 1)),
        lambda s, d: (s, d ^ 2),
        lambda s, d: (s, d ^ 4),
    )
    return [functools.partial(lambda v, p: lax.ppermute(v, AXES, p), p=pairs(c)) for c in changes]


def after(value, *others):
    return lax.optimization_barrier((value, *others))[0]


def gather(shard, over_x, over_y, along_z):
    own, x, y, xy = [shard] + [None] * 3, [None] * 4, [None] * 4, [None] * 4
    x[0], y[0], own[1] = over_x(own[0]), over_y(own[0]), along_z(own[0])
    own[1] = after(own[1], x[0], y[0])
    xy[0], y[1], own[2] = over_x(y[0]), over_y(own[1]), along_z(own[1])
    x[1], y[2], own[3] = over_x(own[1]), over_y(own[2]), along_z(own[2])
    own[3] = after(own[3], xy[0], y[1])
    x[3], y[3], xy[1] = over_x(own[3]), over_y(own[3]), along_z(xy[0])
    x[2] = over_x(after(own[2], x[1]))
    xy[3], xy[2] = over_y(x[3]), along_z(xy[1])
    return own + y, x + xy


def add(*values):
    return sum(v.astype(F32) for v in values)


def scatter(slot0, slot1, dgain, over_x, over_y, along_z):
    own, y, x, xy = slot0[:4], slot0[4:], slot1[:4], slot1[4:]

    def total(*values):
        return add(*values).astype(BF16)

    xy2, xy3, x2 = along_z(xy[2]), over_y(xy[3]), over_x(x[2])
    c3, e1 = total(x[3], xy3), total(xy[1], xy2)
    c3, e1, y3 = lax.optimization_barrier((c3, e1, y[3]))
    y3, c3, e1 = over_y(y3), over_x(c3), along_z(e1)
    s3, e0 = total(own[3], c3, y3), total(xy[0], e1)
    y2, s3, x1 = over_y(after(y[2], xy3, x2)), along_z(s3), over_x(after(x[1], x2))
    s2 = total(own[2], x2, y2, s3)
    e0, y1, s2 = over_x(e0), over_y(after(y[1], y3)), along_z(s2)
    s1, b0 = total(own[1], x1, y1, s2), total(y[0], e0)
    s1 = after(s1, dgain)
    return add(own[0], over_x(after(x[0], c3)), over_y(b0), along_z(s1))


def on_chip_relay(h_forward, h_reverse, weights, gains):
    other_core, over_x, over_y, along_z, z_near, z_far = moves_between()
    tokens, width = h_forward.shape[2:]
    rows, latent = weights.shape[1:]
    x_fwd, x_rev = h_forward[0, 0], other_core(h_reverse[0, 0])
    both_gains = jnp.concatenate([gains, over_x(gains)], axis=0)
    shards = gather(weights[0], over_x, over_y, along_z)

    one = jax.ShapeDtypeStruct((tokens, width), BF16)
    matrix = jax.ShapeDtypeStruct((width, latent), BF16)
    saved_c = jax.ShapeDtypeStruct((tokens, latent), F32)
    saved_p = jax.ShapeDtypeStruct((tokens, tokens), F32)
    dgains = jax.ShapeDtypeStruct((1, latent), F32)
    dcs = jax.ShapeDtypeStruct((tokens, latent), BF16)
    piece = jax.ShapeDtypeStruct((rows, latent), BF16)
    product = 2 * tokens * width * latent

    x1, x2, w, c1, p1 = (x_fwd, x_rev), [None] * 2, [None] * 2, [None] * 2, [None] * 2
    for slot in range(2):
        u, w[slot], c1[slot], p1[slot] = kernel_call(
            functools.partial(first_block, slot), (*shards[slot], both_gains, x1[slot]),
            [one, matrix, saved_c, saved_p], flops=2 * product,
        )
        x2[slot] = other_core(u)
    cot, dc2, dg2 = [None] * 2, [None] * 2, [None] * 2
    for chain in range(2):
        e, dc2[chain], dg2[chain] = kernel_call(
            functools.partial(second_block, chain), (both_gains, x2[chain], *w), [one, dcs, dgains],
            [pltpu.VMEM((tokens, width), BF16), pltpu.VMEM((tokens, latent), F32)], 4 * product,
        )
        cot[chain] = other_core(e)
    parts, dgain, grads = [None] * 2, [None] * 2, [None] * 2
    dc1 = [None] * 2
    for slot in range(2):
        dc1[slot], dgain[slot], *parts[slot] = kernel_call(
            functools.partial(first_weight_grad, slot),
            (both_gains, x1[slot], c1[slot], p1[slot], cot[slot], *x2, *dc2, *dg2), [dcs, dgains] + [piece] * 8,
            [pltpu.VMEM((width, latent), BF16), pltpu.VMEM((2 * tokens, latent), BF16)], 4 * product,
        )
    for slot in range(2):
        (grads[slot],) = kernel_call(first_input_grad, (cot[slot], p1[slot], dc1[slot], w[slot]), [one], flops=2 * product)
    dgain = dgain[0] + over_x(dgain[1])
    dgain = dgain + over_y(dgain)
    dgain = dgain + z_near(dgain)
    dgain = dgain + z_far(dgain)
    grad_weights = scatter(*parts, dgain, over_x, over_y, along_z)
    return grads[0][None, None], other_core(grads[1])[None, None], grad_weights[None], dgain


def from_partner(value, axis, apart):
    mask = 2**apart
    pairs = [(source, source ^ mask) for source in range(lax.axis_size(axis))]
    return lax.ppermute(value, axis, pairs)


def passed_along(value, axis, by):
    devices = lax.axis_size(axis)
    return lax.ppermute(value, axis, [(i, (i + by) % devices) for i in range(devices)])


def group_forward(x, w, g):
    c = jnp.dot(x, w, preferred_element_type=jnp.float32)
    inv = lax.rsqrt(jnp.mean(c * c, axis=-1, keepdims=True) + EPS)
    normed = (c * inv * g.astype(jnp.float32)).astype(jnp.bfloat16)
    scale = 3.0 / c.shape[-1]
    scores = jnp.dot(normed, normed.T, preferred_element_type=jnp.float32) * scale
    count = x.shape[0]
    rows = lax.broadcasted_iota(jnp.int32, (count, count), 0)
    cols = lax.broadcasted_iota(jnp.int32, (count, count), 1)
    scores = jnp.where(cols <= rows, scores, -1e30)
    top = jnp.max(scores, axis=-1, keepdims=True)
    expo = jnp.exp(scores - top)
    probs = expo / jnp.sum(expo, axis=-1, keepdims=True)
    probs_b = probs.astype(jnp.bfloat16)
    mixed = jnp.dot(probs_b, x, preferred_element_type=jnp.float32)
    out = (x.astype(jnp.float32) + mixed).astype(jnp.bfloat16)
    return (out, (c, inv, normed, probs, probs_b))


def group_backward(x, w, g, saved, grad_out):
    c, inv, normed, probs, probs_b = saved
    scale = 3.0 / c.shape[-1]
    dx = grad_out.astype(jnp.float32) + jnp.dot(
        probs_b.T, grad_out, preferred_element_type=jnp.float32
    )
    dprobs = jnp.dot(grad_out, x.T, preferred_element_type=jnp.float32)
    dscores = probs * (dprobs - jnp.sum(dprobs * probs, axis=-1, keepdims=True))
    dscores_b = (dscores * scale).astype(jnp.bfloat16)
    dnormed = jnp.dot(dscores_b, normed, preferred_element_type=jnp.float32) + jnp.dot(
        dscores_b.T, normed, preferred_element_type=jnp.float32
    )
    dgain = jnp.sum(dnormed * c * inv, axis=0)
    dhat = dnormed * g.astype(jnp.float32)
    dc = inv * dhat - c * (inv * inv * inv) * jnp.mean(dhat * c, axis=-1, keepdims=True)
    dc_b = dc.astype(jnp.bfloat16)
    dx = dx + jnp.dot(dc_b, w.T, preferred_element_type=jnp.float32)
    dw = jnp.dot(x.T, dc_b, preferred_element_type=jnp.float32)
    return (dx, dw, dgain)


def twin_copy(pair):
    for bit in range(lax.axis_size("section").bit_length() - 1):
        pair = from_partner((pair[0], pair[1]), "section", bit)
    return (pair[0], pair[1])


def grad_twin(pair):
    for bit in range(lax.axis_size("section").bit_length() - 1):
        pair = (
            from_partner(pair[0].astype(jnp.bfloat16), "section", bit).astype(jnp.float32),
            from_partner(pair[1].astype(jnp.bfloat16), "section", bit).astype(jnp.float32),
        )
    return (pair[0], pair[1])


def neighbour(values, offset):
    return passed_along(values, "section", offset)


def sections_apart(h_forward, h_reverse, weights, gains):
    shard = weights[0]
    gain = gains[0]
    twin_shard, twin_gain = twin_copy((shard, gain))
    own, twin = (
        lax.all_gather(shard, "dp", axis=0, tiled=True),
        lax.all_gather(twin_shard, "dp", axis=0, tiled=True),
    )
    x_fwd = h_forward[0, 0]
    x_rev = h_reverse[0, 0]
    u_fwd, saved_f1 = group_forward(x_fwd, own, gain)
    u_rev, saved_r1 = group_forward(x_rev, twin, twin_gain)
    in_fwd = neighbour(u_fwd, 1)
    in_rev = neighbour(u_rev, -1)
    v_fwd, saved_f2 = group_forward(in_fwd, own, gain)
    v_rev, saved_r2 = group_forward(in_rev, twin, twin_gain)
    din_fwd, dw_f2, dg_f2 = group_backward(in_fwd, own, gain, saved_f2, v_fwd)
    din_rev, dw_r2, dg_r2 = group_backward(in_rev, twin, twin_gain, saved_r2, v_rev)
    back_fwd = neighbour(din_fwd.astype(jnp.bfloat16), -1)
    back_rev = neighbour(din_rev.astype(jnp.bfloat16), 1)
    dh_fwd, dw_f1, dg_f1 = group_backward(x_fwd, own, gain, saved_f1, back_fwd)
    dh_rev, dw_r1, dg_r1 = group_backward(x_rev, twin, twin_gain, saved_r1, back_rev)
    share_fwd, share_rev = (
        lax.psum_scatter(
            (dw_f1 + dw_f2).astype(jnp.bfloat16), "dp", scatter_dimension=0, tiled=True
        ).astype(jnp.float32),
        lax.psum_scatter(
            (dw_r1 + dw_r2).astype(jnp.bfloat16), "dp", scatter_dimension=0, tiled=True
        ).astype(jnp.float32),
    )
    gsum_fwd, gsum_rev = lax.psum((dg_f1 + dg_f2, dg_r1 + dg_r2), "dp")
    mirror_w, mirror_g = grad_twin((share_rev, gsum_rev))
    grad_weights = (share_fwd + mirror_w)[None]
    grad_gains = (gsum_fwd + mirror_g)[None]
    return (
        dh_fwd.astype(jnp.bfloat16)[None, None],
        dh_rev.astype(jnp.bfloat16)[None, None],
        grad_weights,
        grad_gains,
    )


def solution(mesh):
    in_specs = (
        P("section", "dp", None, None),
        P("section", "dp", None, None),
        P("section", "dp", None),
        P("section", None),
    )
    out_specs = (
        P("section", "dp", None, None),
        P("section", "dp", None, None),
        P("section", "dp", None),
        P("section", None),
    )
    on_chip = (mesh.shape["section"], mesh.shape["dp"]) == (4, 8)
    on_device = on_chip_relay if on_chip else sections_apart
    return jax.shard_map(
        on_device, mesh=mesh, in_specs=in_specs, out_specs=out_specs, check_vma=False
    )
```

```python
import functools

import jax
import jax.numpy as jnp
from jax import lax
from jax.experimental import pallas as pl
from jax.experimental.pallas import tpu as pltpu
from jax.sharding import PartitionSpec as P

EPS = 1e-06
AXES = ("section", "dp")
BF16 = jnp.bfloat16
F32 = jnp.float32
CHUNK = 512
TAIL = 16
VMEM_LIMIT = 40 * 1024 * 1024


def matmul(a, b):
    return jnp.dot(a, b, preferred_element_type=F32)


def matmul_nt(a, b):
    return lax.dot_general(a, b, (((1,), (1,)), ((), ())), preferred_element_type=F32)


def matmul_tn(a, b):
    return lax.dot_general(a, b, (((0,), (0,)), ((), ())), preferred_element_type=F32)


def latent_norm(c, g):
    inv = lax.rsqrt(jnp.mean(c * c, axis=-1, keepdims=True) + EPS)
    return inv, (c * inv * g.astype(F32)).astype(BF16)


def attention(normed, width):
    scores = matmul_nt(normed, normed) * (3.0 / width)
    rows = lax.broadcasted_iota(jnp.int32, scores.shape, 0)
    cols = lax.broadcasted_iota(jnp.int32, scores.shape, 1)
    scores = jnp.where(cols <= rows, scores, -1e30)
    expo = jnp.exp(scores - jnp.max(scores, axis=-1, keepdims=True))
    return expo / jnp.sum(expo, axis=-1, keepdims=True)


def column_chunks(width):
    return [slice(at, at + CHUNK) for at in range(0, width, CHUNK)]


def mix_into(out_ref, x_ref, probs_b):
    for cols in column_chunks(x_ref.shape[-1]):
        x = x_ref[:, cols]
        out_ref[:, cols] = (x.astype(F32) + matmul(probs_b, x)).astype(BF16)


def score_grad(dy_ref, x_ref):
    total = None
    for cols in column_chunks(x_ref.shape[-1]):
        part = matmul_nt(dy_ref[:, cols], x_ref[:, cols])
        total = part if total is None else total + part
    return total


def latent_grad(dprobs, probs, c, inv, normed, g):
    scale = 3.0 / c.shape[-1]
    dscores = probs * (dprobs - jnp.sum(dprobs * probs, axis=-1, keepdims=True))
    dscores_b = (dscores * scale).astype(BF16)
    dnormed = matmul(dscores_b, normed) + matmul_tn(dscores_b, normed)
    dgain = jnp.sum(dnormed * c * inv, axis=0, keepdims=True)
    dhat = dnormed * g.astype(F32)
    dc = inv * dhat - c * (inv * inv * inv) * jnp.mean(dhat * c, axis=-1, keepdims=True)
    return dc.astype(BF16), dgain


def input_grad(out_ref, dy_ref, probs_b, dc_b, w_ref):
    for cols in column_chunks(dy_ref.shape[-1]):
        dy = dy_ref[:, cols]
        dx = dy.astype(F32) + matmul_tn(probs_b, dy) + matmul_nt(dc_b, w_ref[cols, :])
        out_ref[:, cols] = dx.astype(BF16)


def ring_place(value):
    return value ^ (value >> 1)


def shard_row(dy, steps, rows):
    dp = lax.axis_index("dp")
    place = (ring_place(dp >> 1) + steps) & 3
    return pl.multiple_of((ring_place(place) * 2 + ((dp & 1) ^ dy)) * rows, 16)


def slot_of(chain):
    return chain ^ 1 ^ (lax.axis_index("section") & 1)


def first_block(slot, *refs):
    pieces, (gain_ref, x_ref, u_ref, w_ref, c_ref, p_ref) = refs[:8], refs[8:]
    rows = pieces[0].shape[0]
    for at, piece in enumerate(pieces):
        w_ref[pl.ds(shard_row(at // 4, 4 - at % 4, rows), rows), :] = piece[...]
    c = matmul(x_ref[...], w_ref[...])
    _, normed = latent_norm(c, gain_ref[slot : slot + 1, :])
    probs = attention(normed, c.shape[-1])
    c_ref[...] = c
    p_ref[...] = probs
    mix_into(u_ref, x_ref, probs.astype(BF16))


def second_block(chain, gain_ref, x_ref, w0_ref, w1_ref, e_ref, dc_ref, dg_ref, v_ref, c_ref):
    slot = slot_of(chain)
    g = jnp.where(slot == 0, gain_ref[0:1, :].astype(F32), gain_ref[1:2, :].astype(F32))
    for at, w_ref in enumerate((w0_ref, w1_ref)):

        @pl.when(slot == at)
        def _(w_ref=w_ref):
            c_ref[...] = matmul(x_ref[...], w_ref[...])

    c = c_ref[...]
    inv, normed = latent_norm(c, g)
    probs = attention(normed, c.shape[-1])
    probs_b = probs.astype(BF16)
    mix_into(v_ref, x_ref, probs_b)
    dc_b, dgain = latent_grad(score_grad(v_ref, x_ref), probs, c, inv, normed, g)
    dc_ref[...] = dc_b
    dg_ref[...] = dgain
    for at, w_ref in enumerate((w0_ref, w1_ref)):

        @pl.when(slot == at)
        def _(w_ref=w_ref):
            input_grad(e_ref, v_ref, probs_b, dc_b, w_ref)


def first_weight_grad(slot, *refs):
    gain_ref, x_ref, c_ref, p_ref, cot_ref, x2a_ref, x2b_ref, dc2a_ref, dc2b_ref, dg2a_ref, dg2b_ref = refs[:11]
    dc_ref, pieces, (dw_ref, dcs_ref, dg_ref) = refs[11], refs[12:20], refs[20:]
    tokens, rows = x_ref.shape[0], pieces[0].shape[0] - TAIL
    g = gain_ref[slot : slot + 1, :]
    c, probs = c_ref[...], p_ref[...]
    inv, normed = latent_norm(c, g)
    dc_b, dgain = latent_grad(score_grad(cot_ref, x_ref), probs, c, inv, normed, g)
    dc_ref[...] = dc_b
    dcs_ref[:tokens, :] = dc_b
    for chain, x2_ref, dc2_ref, dg2_ref in ((0, x2a_ref, dc2a_ref, dg2a_ref), (1, x2b_ref, dc2b_ref, dg2b_ref)):

        @pl.when(slot_of(chain) == slot)
        def _(x2_ref=x2_ref, dc2_ref=dc2_ref, dg2_ref=dg2_ref):
            dg_ref[...] = dgain + dg2_ref[...]
            dcs_ref[tokens:, :] = dc2_ref[...]
            for cols in column_chunks(x_ref.shape[-1]):
                x = jnp.concatenate([x_ref[:, cols], x2_ref[:, cols]], axis=0)
                dw_ref[cols, :] = matmul_tn(x, dcs_ref[...]).astype(BF16)

    tail = split_tail(dg_ref[...])
    for at, piece in enumerate(pieces):
        piece[:rows, :] = dw_ref[pl.ds(shard_row(at // 4, 4 - at % 4, rows), rows), :]
        piece[rows:, :] = tail


def split_tail(dgain):
    high = dgain.astype(BF16).astype(F32)
    at = lax.broadcasted_iota(jnp.int32, (TAIL, dgain.shape[-1]), 0)
    return jnp.where(at == 0, high, jnp.where(at == 1, dgain - high, 0.0)).astype(BF16)


def sum_rows(refs):
    return sum(ref[:-TAIL, :].astype(F32) for ref in refs)


def sum_tail(refs):
    tail = sum(ref[-TAIL:, :].astype(F32) for ref in refs)
    return tail[0:1, :] + tail[1:2, :]


def partial_sum(*refs):
    *ins, out_ref = refs
    out_ref[:-TAIL, :] = sum_rows(ins).astype(BF16)
    out_ref[-TAIL:, :] = split_tail(sum_tail(ins))


def final_sum(*refs):
    *ins, out_ref, dg_ref = refs
    out_ref[...] = sum_rows(ins)
    dg_ref[...] = sum_tail(ins)


def first_input_grad(cot_ref, p_ref, dc_ref, w_ref, out_ref):
    input_grad(out_ref, cot_ref, p_ref[...].astype(BF16), dc_ref[...], w_ref)


def store(value_ref, out_ref):
    pltpu.sync_copy(value_ref, out_ref)


def kernel_call(body, args, outs, scratch=(), flops=0, out_space=pltpu.VMEM):
    local = pl.BlockSpec(memory_space=pltpu.VMEM)
    return pl.pallas_call(
        body,
        out_shape=outs,
        in_specs=[local] * len(args),
        out_specs=[pl.BlockSpec(memory_space=out_space)] * len(outs),
        scratch_shapes=scratch,
        compiler_params=pltpu.CompilerParams(vmem_limit_bytes=VMEM_LIMIT),
        name=getattr(body, "func", body).__name__,
        cost_estimate=pl.CostEstimate(flops=flops, bytes_accessed=4 << 20, transcendentals=0),
    )(*args)


GATHER = (
    ("Y0", "y", "O0", ()),
    ("O3", "r", "O0", ()),
    ("X0", "x", "O0", ()),
    ("O1", "z", "O0", ()),
    ("D0", "x", "Y0", ("G", "H")),
    ("Y3", "y", "O3", ()),
    ("O2", "r", "O3", ("Y0",)),
    ("X3", "x", "O3", ("Y0",)),
    ("Y1", "y", "O1", ("X0", "O3", "Y0")),
    ("D1", "z", "D0", ("X0", "O3", "Y0")),
    ("X1", "x", "O1", ("X0", "O3", "Y0")),
    ("Y2", "y", "O2", ("D0", "O1", "X0")),
    ("D3", "r", "D0", ("Y3", "O1", "X0")),
    ("X2", "x", "O2", ("Y3", "D0", "O1")),
    ("D2", "z", "D1", ("Y1", "X3", "O2")),
)
SCATTER = (
    ("D2", "z", "D1", ()),
    ("Y2", "y", "O2", ()),
    ("D3", "x", "Y3", ()),
    ("R", "", "", ()),
    ("Y1", "y", "O1", ()),
    ("X2", "x", "O2", ()),
    ("D1", "z", "D0", ()),
    ("Y3", "y", "O3", ("D2",)),
    ("X3", "x", "O3", ("D3", "Y2", "D2")),
    ("O2", "z", "O1", ("R", "D3", "D2")),
    ("D0", "y", "X0", ("Y1", "R", "D3")),
    ("X1", "x", "O1", ("X2", "Y1", "R")),
    ("F", "", "", ("D1", "X2", "Y1")),
    ("O3", "r", "O0", ("D1", "X2", "Y1")),
    ("Y0", "y", "O0", ("Y3", "D1", "X2")),
    ("X0", "x", "O0", ("F", "X3", "Y3")),
    ("O1", "z", "O0", ("F", "X3", "Y3")),
)
FIRST_AFTER = ("D3", "Y2")
PLACES = tuple(tuple(column + str(k) for column in columns for k in range(4)) for columns in ("OY", "XD"))
BACK = {"x": "x", "y": "y", "z": "r", "r": "z"}


def moves_between():
    def pairs(change):
        found = []
        for i in range(32):
            s, d = divmod(i, 8)
            to_s, to_d = change(s, d)
            found.append((i, to_s * 8 + to_d))
        return found

    following = {0: 1, 1: 3, 3: 2, 2: 0}
    last = {after: before for before, after in following.items()}
    changes = {
        "core": lambda s, d: (s ^ 1, d),
        "x": lambda s, d: (s ^ 2, d),
        "y": lambda s, d: (s, d ^ 1),
        "z": lambda s, d: (s, following[d >> 1] * 2 + (d & 1)),
        "r": lambda s, d: (s, last[d >> 1] * 2 + (d & 1)),
    }
    return {name: functools.partial(lambda v, p: lax.ppermute(v, AXES, p), p=pairs(c)) for name, c in changes.items()}


def after(value, others):
    return lax.optimization_barrier((value, *others))[0] if others else value


def gather(held, moves):
    for place, way, source, earlier in GATHER:
        held[place] = moves[way](after(held[source], [held[name] for name in earlier]))


def scatter(parts, beside, moves):
    rows, latent = parts["O0"].shape
    piece = jax.ShapeDtypeStruct((rows, latent), BF16)
    sums = [jax.ShapeDtypeStruct((rows - TAIL, latent), F32), jax.ShapeDtypeStruct((1, latent), F32)]
    into, held = {}, {}
    for place, _, source, _ in SCATTER:
        into.setdefault(source, []).append(place)
    for place, way, _, earlier in SCATTER:
        earlier = [held[name] for name in earlier]
        if place in beside:
            held[place] = beside[place](earlier)
            continue
        value = parts[place]
        if place in into:
            value = kernel_call(partial_sum, (value, *[held[name] for name in into[place]]), [piece])[0]
        held[place] = moves[BACK[way]](after(value, earlier))
    sums = kernel_call(final_sum, (parts["O0"], *[held[name] for name in into["O0"]]), sums)
    return sums, held


def on_chip_relay(h_forward, h_reverse, weights, gains):
    moves = moves_between()
    other_core = moves["core"]
    tokens, width = h_forward.shape[2:]
    rows, latent = weights.shape[1:]
    x_fwd, x_rev = h_forward[0, 0], other_core(h_reverse[0, 0])
    both_gains = jnp.concatenate([gains, moves["x"](gains)], axis=0)
    held = {"O0": weights[0], "G": both_gains, "H": x_rev}
    gather(held, moves)

    one = jax.ShapeDtypeStruct((tokens, width), BF16)
    matrix = jax.ShapeDtypeStruct((width, latent), BF16)
    saved_c = jax.ShapeDtypeStruct((tokens, latent), F32)
    saved_p = jax.ShapeDtypeStruct((tokens, tokens), F32)
    dgains = jax.ShapeDtypeStruct((1, latent), F32)
    dcs = jax.ShapeDtypeStruct((tokens, latent), BF16)
    piece = jax.ShapeDtypeStruct((rows + TAIL, latent), BF16)
    product = 2 * tokens * width * latent

    x1, x2, w, c1, p1 = (x_fwd, x_rev), [None] * 2, [None] * 2, [None] * 2, [None] * 2
    for slot in range(2):
        gain = after(both_gains, [c1[0]] if slot else [held[name] for name in FIRST_AFTER])
        u, w[slot], c1[slot], p1[slot] = kernel_call(
            functools.partial(first_block, slot), (*[held[name] for name in PLACES[slot]], gain, x1[slot]),
            [one, matrix, saved_c, saved_p], flops=2 * product,
        )
        x2[slot] = other_core(u)
    cot, dc2, dg2 = [None] * 2, [None] * 2, [None] * 2
    for chain in range(2):
        gain = after(both_gains, [dc2[0]] if chain else [])
        e, dc2[chain], dg2[chain] = kernel_call(
            functools.partial(second_block, chain), (gain, x2[chain], *w), [one, dcs, dgains],
            [pltpu.VMEM((tokens, width), BF16), pltpu.VMEM((tokens, latent), F32)], 4 * product,
        )
        cot[chain] = other_core(e)
    parts, dc1 = [None] * 2, [None] * 2
    for slot in range(2):
        dc1[slot], *parts[slot] = kernel_call(
            functools.partial(first_weight_grad, slot),
            (both_gains, x1[slot], c1[slot], p1[slot], cot[slot], *x2, *dc2, *dg2), [dcs] + [piece] * 8,
            [pltpu.VMEM((width, latent), BF16), pltpu.VMEM((2 * tokens, latent), BF16), pltpu.VMEM((1, latent), F32)],
            4 * product,
        )

    def input_grads(slot, earlier):
        args = (after(cot[slot], earlier), p1[slot], dc1[slot], w[slot])
        (grad,) = kernel_call(first_input_grad, args, [one], flops=2 * product)
        return kernel_call(store, (other_core(grad),), [one], out_space=pl.ANY)[0] if slot else grad

    beside = {"F": functools.partial(input_grads, 0), "R": functools.partial(input_grads, 1)}
    parts = {name: part for slot in range(2) for name, part in zip(PLACES[slot], parts[slot])}
    (grad_weights, dgain), held = scatter(parts, beside, moves)
    return held["F"][None, None], held["R"][None, None], grad_weights[None], dgain


def from_partner(value, axis, apart):
    mask = 2**apart
    pairs = [(source, source ^ mask) for source in range(lax.axis_size(axis))]
    return lax.ppermute(value, axis, pairs)


def passed_along(value, axis, by):
    devices = lax.axis_size(axis)
    return lax.ppermute(value, axis, [(i, (i + by) % devices) for i in range(devices)])


def group_forward(x, w, g):
    c = jnp.dot(x, w, preferred_element_type=jnp.float32)
    inv = lax.rsqrt(jnp.mean(c * c, axis=-1, keepdims=True) + EPS)
    normed = (c * inv * g.astype(jnp.float32)).astype(jnp.bfloat16)
    scale = 3.0 / c.shape[-1]
    scores = jnp.dot(normed, normed.T, preferred_element_type=jnp.float32) * scale
    count = x.shape[0]
    rows = lax.broadcasted_iota(jnp.int32, (count, count), 0)
    cols = lax.broadcasted_iota(jnp.int32, (count, count), 1)
    scores = jnp.where(cols <= rows, scores, -1e30)
    top = jnp.max(scores, axis=-1, keepdims=True)
    expo = jnp.exp(scores - top)
    probs = expo / jnp.sum(expo, axis=-1, keepdims=True)
    probs_b = probs.astype(jnp.bfloat16)
    mixed = jnp.dot(probs_b, x, preferred_element_type=jnp.float32)
    out = (x.astype(jnp.float32) + mixed).astype(jnp.bfloat16)
    return (out, (c, inv, normed, probs, probs_b))


def group_backward(x, w, g, saved, grad_out):
    c, inv, normed, probs, probs_b = saved
    scale = 3.0 / c.shape[-1]
    dx = grad_out.astype(jnp.float32) + jnp.dot(
        probs_b.T, grad_out, preferred_element_type=jnp.float32
    )
    dprobs = jnp.dot(grad_out, x.T, preferred_element_type=jnp.float32)
    dscores = probs * (dprobs - jnp.sum(dprobs * probs, axis=-1, keepdims=True))
    dscores_b = (dscores * scale).astype(jnp.bfloat16)
    dnormed = jnp.dot(dscores_b, normed, preferred_element_type=jnp.float32) + jnp.dot(
        dscores_b.T, normed, preferred_element_type=jnp.float32
    )
    dgain = jnp.sum(dnormed * c * inv, axis=0)
    dhat = dnormed * g.astype(jnp.float32)
    dc = inv * dhat - c * (inv * inv * inv) * jnp.mean(dhat * c, axis=-1, keepdims=True)
    dc_b = dc.astype(jnp.bfloat16)
    dx = dx + jnp.dot(dc_b, w.T, preferred_element_type=jnp.float32)
    dw = jnp.dot(x.T, dc_b, preferred_element_type=jnp.float32)
    return (dx, dw, dgain)


def twin_copy(pair):
    for bit in range(lax.axis_size("section").bit_length() - 1):
        pair = from_partner((pair[0], pair[1]), "section", bit)
    return (pair[0], pair[1])


def grad_twin(pair):
    for bit in range(lax.axis_size("section").bit_length() - 1):
        pair = (
            from_partner(pair[0].astype(jnp.bfloat16), "section", bit).astype(jnp.float32),
            from_partner(pair[1].astype(jnp.bfloat16), "section", bit).astype(jnp.float32),
        )
    return (pair[0], pair[1])


def neighbour(values, offset):
    return passed_along(values, "section", offset)


def sections_apart(h_forward, h_reverse, weights, gains):
    shard = weights[0]
    gain = gains[0]
    twin_shard, twin_gain = twin_copy((shard, gain))
    own, twin = (
        lax.all_gather(shard, "dp", axis=0, tiled=True),
        lax.all_gather(twin_shard, "dp", axis=0, tiled=True),
    )
    x_fwd = h_forward[0, 0]
    x_rev = h_reverse[0, 0]
    u_fwd, saved_f1 = group_forward(x_fwd, own, gain)
    u_rev, saved_r1 = group_forward(x_rev, twin, twin_gain)
    in_fwd = neighbour(u_fwd, 1)
    in_rev = neighbour(u_rev, -1)
    v_fwd, saved_f2 = group_forward(in_fwd, own, gain)
    v_rev, saved_r2 = group_forward(in_rev, twin, twin_gain)
    din_fwd, dw_f2, dg_f2 = group_backward(in_fwd, own, gain, saved_f2, v_fwd)
    din_rev, dw_r2, dg_r2 = group_backward(in_rev, twin, twin_gain, saved_r2, v_rev)
    back_fwd = neighbour(din_fwd.astype(jnp.bfloat16), -1)
    back_rev = neighbour(din_rev.astype(jnp.bfloat16), 1)
    dh_fwd, dw_f1, dg_f1 = group_backward(x_fwd, own, gain, saved_f1, back_fwd)
    dh_rev, dw_r1, dg_r1 = group_backward(x_rev, twin, twin_gain, saved_r1, back_rev)
    share_fwd, share_rev = (
        lax.psum_scatter(
            (dw_f1 + dw_f2).astype(jnp.bfloat16), "dp", scatter_dimension=0, tiled=True
        ).astype(jnp.float32),
        lax.psum_scatter(
            (dw_r1 + dw_r2).astype(jnp.bfloat16), "dp", scatter_dimension=0, tiled=True
        ).astype(jnp.float32),
    )
    gsum_fwd, gsum_rev = lax.psum((dg_f1 + dg_f2, dg_r1 + dg_r2), "dp")
    mirror_w, mirror_g = grad_twin((share_rev, gsum_rev))
    grad_weights = (share_fwd + mirror_w)[None]
    grad_gains = (gsum_fwd + mirror_g)[None]
    return (
        dh_fwd.astype(jnp.bfloat16)[None, None],
        dh_rev.astype(jnp.bfloat16)[None, None],
        grad_weights,
        grad_gains,
    )


def solution(mesh):
    in_specs = (
        P("section", "dp", None, None),
        P("section", "dp", None, None),
        P("section", "dp", None),
        P("section", None),
    )
    out_specs = (
        P("section", "dp", None, None),
        P("section", "dp", None, None),
        P("section", "dp", None),
        P("section", None),
    )
    on_chip = (mesh.shape["section"], mesh.shape["dp"]) == (4, 8)
    on_device = on_chip_relay if on_chip else sections_apart
    return jax.shard_map(
        on_device, mesh=mesh, in_specs=in_specs, out_specs=out_specs, check_vma=False
    )
```

```python
import functools

import jax
import jax.numpy as jnp
from jax import lax
from jax.experimental import pallas as pl
from jax.experimental.pallas import tpu as pltpu
from jax.sharding import PartitionSpec as P

EPS = 1e-06
AXES = ("section", "dp")
BF16 = jnp.bfloat16
F32 = jnp.float32
CHUNK = 512
TAIL = 16
VMEM_LIMIT = 40 * 1024 * 1024


def matmul(a, b):
    return jnp.dot(a, b, preferred_element_type=F32)


def matmul_nt(a, b):
    return lax.dot_general(a, b, (((1,), (1,)), ((), ())), preferred_element_type=F32)


def matmul_tn(a, b):
    return lax.dot_general(a, b, (((0,), (0,)), ((), ())), preferred_element_type=F32)


def latent_norm(c, g):
    inv = lax.rsqrt(jnp.mean(c * c, axis=-1, keepdims=True) + EPS)
    return inv, (c * inv * g.astype(F32)).astype(BF16)


def attention(normed, width):
    scores = matmul_nt(normed, normed) * (3.0 / width)
    rows = lax.broadcasted_iota(jnp.int32, scores.shape, 0)
    cols = lax.broadcasted_iota(jnp.int32, scores.shape, 1)
    scores = jnp.where(cols <= rows, scores, -1e30)
    expo = jnp.exp(scores - jnp.max(scores, axis=-1, keepdims=True))
    return expo / jnp.sum(expo, axis=-1, keepdims=True)


def column_chunks(width):
    return [slice(at, at + CHUNK) for at in range(0, width, CHUNK)]


def mix_into(out_ref, x_ref, probs_b):
    for cols in column_chunks(x_ref.shape[-1]):
        x = x_ref[:, cols]
        out_ref[:, cols] = (x.astype(F32) + matmul(probs_b, x)).astype(BF16)


def score_grad(dy_ref, x_ref):
    total = None
    for cols in column_chunks(x_ref.shape[-1]):
        part = matmul_nt(dy_ref[:, cols], x_ref[:, cols])
        total = part if total is None else total + part
    return total


def latent_grad(dprobs, probs, c, inv, normed, g):
    scale = 3.0 / c.shape[-1]
    dscores = probs * (dprobs - jnp.sum(dprobs * probs, axis=-1, keepdims=True))
    dscores_b = (dscores * scale).astype(BF16)
    dnormed = matmul(dscores_b, normed) + matmul_tn(dscores_b, normed)
    dgain = jnp.sum(dnormed * c * inv, axis=0, keepdims=True)
    dhat = dnormed * g.astype(F32)
    dc = inv * dhat - c * (inv * inv * inv) * jnp.mean(dhat * c, axis=-1, keepdims=True)
    return dc.astype(BF16), dgain


def input_grad(out_ref, dy_ref, probs_b, dc_b, w_ref, after_chunk=None):
    left = jnp.concatenate([probs_b.astype(F32).T.astype(BF16), dc_b], axis=1)
    for at, cols in enumerate(column_chunks(dy_ref.shape[-1])):
        dy = dy_ref[:, cols]
        dx = dy.astype(F32) + matmul(left, jnp.concatenate([dy, w_ref[cols, :].T], axis=0))
        out_ref[:, cols] = dx.astype(BF16)
        if after_chunk is not None:
            after_chunk(at, cols)


def ring_place(value):
    return value ^ (value >> 1)


def shard_row(dy, steps, rows):
    dp = lax.axis_index("dp")
    place = (ring_place(dp >> 1) + steps) & 3
    return pl.multiple_of((ring_place(place) * 2 + ((dp & 1) ^ dy)) * rows, 16)


def slot_of(chain):
    return chain ^ 1 ^ (lax.axis_index("section") & 1)


def place_shards(w_ref, pieces):
    rows = pieces[-1].shape[0]
    for at, piece in enumerate(pieces):
        if piece is not None:
            w_ref[pl.ds(shard_row(at // 4, 4 - at % 4, rows), rows), :] = piece[...]


def first_output(slot, c, gain_ref, x_ref, u_ref, c_ref, p_ref):
    _, normed = latent_norm(c, gain_ref[slot : slot + 1, :])
    probs = attention(normed, c.shape[-1])
    c_ref[...] = c
    p_ref[...] = probs
    mix_into(u_ref, x_ref, probs.astype(BF16))


def first_block_own(own_ref, x_hbm_ref, *refs):
    pieces, (gain_ref, u_ref, w_ref, c_ref, p_ref, x_ref, sems) = refs[:7], refs[7:]
    rows = own_ref.shape[0]
    own = pltpu.make_async_copy(own_ref, w_ref.at[pl.ds(shard_row(0, 0, rows), rows), :], sems.at[0])
    chunks = column_chunks(x_ref.shape[-1])
    loads = [pltpu.make_async_copy(x_hbm_ref.at[:, cols], x_ref.at[:, cols], sems.at[1 + i]) for i, cols in enumerate(chunks)]
    for load in (own, *loads):
        load.start()
    place_shards(w_ref, (None, *pieces))
    own.wait()
    c = 0.0
    for load, cols in zip(loads, chunks):
        load.wait()
        c = c + matmul(x_ref[:, cols], w_ref[cols, :])
    first_output(0, c, gain_ref, x_ref, u_ref, c_ref, p_ref)


def first_block_other(*refs):
    pieces, (gain_ref, x_ref, u_ref, w_ref, c_ref, p_ref) = refs[:8], refs[8:]
    place_shards(w_ref, pieces)
    first_output(1, matmul(x_ref[...], w_ref[...]), gain_ref, x_ref, u_ref, c_ref, p_ref)


def second_block(chain, gain_ref, x_ref, w0_ref, w1_ref, e_ref, dc_ref, dg_ref, v_ref, c_ref):
    slot = slot_of(chain)
    g = jnp.where(slot == 0, gain_ref[0:1, :].astype(F32), gain_ref[1:2, :].astype(F32))
    for at, w_ref in enumerate((w0_ref, w1_ref)):

        @pl.when(slot == at)
        def _(w_ref=w_ref):
            c_ref[...] = matmul(x_ref[...], w_ref[...])

    c = c_ref[...]
    inv, normed = latent_norm(c, g)
    probs = attention(normed, c.shape[-1])
    probs_b = probs.astype(BF16)
    mix_into(v_ref, x_ref, probs_b)
    dc_b, dgain = latent_grad(score_grad(v_ref, x_ref), probs, c, inv, normed, g)
    dc_ref[...] = dc_b
    dg_ref[...] = dgain
    for at, w_ref in enumerate((w0_ref, w1_ref)):

        @pl.when(slot == at)
        def _(w_ref=w_ref):
            input_grad(e_ref, v_ref, probs_b, dc_b, w_ref)


def first_weight_grad(slot, *refs):
    gain_ref, x_ref, c_ref, p_ref, cot_ref, x2a_ref, x2b_ref, dc2a_ref, dc2b_ref, dg2a_ref, dg2b_ref = refs[:11]
    dc_ref, pieces, (dw_ref, dcs_ref, dg_ref) = refs[11], refs[12:20], refs[20:]
    tokens, rows = x_ref.shape[0], pieces[0].shape[0] - TAIL
    g = gain_ref[slot : slot + 1, :]
    c, probs = c_ref[...], p_ref[...]
    inv, normed = latent_norm(c, g)
    dc_b, dgain = latent_grad(score_grad(cot_ref, x_ref), probs, c, inv, normed, g)
    dc_ref[...] = dc_b
    dcs_ref[:tokens, :] = dc_b
    for chain, x2_ref, dc2_ref, dg2_ref in ((0, x2a_ref, dc2a_ref, dg2a_ref), (1, x2b_ref, dc2b_ref, dg2b_ref)):

        @pl.when(slot_of(chain) == slot)
        def _(x2_ref=x2_ref, dc2_ref=dc2_ref, dg2_ref=dg2_ref):
            dg_ref[...] = dgain + dg2_ref[...]
            dcs_ref[tokens:, :] = dc2_ref[...]
            for cols in column_chunks(x_ref.shape[-1]):
                x = jnp.concatenate([x_ref[:, cols], x2_ref[:, cols]], axis=0)
                dw_ref[cols, :] = matmul_tn(x, dcs_ref[...]).astype(BF16)

    tail = split_tail(dg_ref[...])
    for at, piece in enumerate(pieces):
        piece[:rows, :] = dw_ref[pl.ds(shard_row(at // 4, 4 - at % 4, rows), rows), :]
        piece[rows:, :] = tail


def split_tail(dgain):
    high = dgain.astype(BF16).astype(F32)
    at = lax.broadcasted_iota(jnp.int32, (TAIL, dgain.shape[-1]), 0)
    return jnp.where(at == 0, high, jnp.where(at == 1, dgain - high, 0.0)).astype(BF16)


def sum_rows(refs):
    return sum(ref[:-TAIL, :].astype(F32) for ref in refs)


def sum_tail(refs):
    tail = sum(ref[-TAIL:, :].astype(F32) for ref in refs)
    return tail[0:1, :] + tail[1:2, :]


def partial_sum(*refs):
    *ins, out_ref = refs
    out_ref[:-TAIL, :] = sum_rows(ins).astype(BF16)
    out_ref[-TAIL:, :] = split_tail(sum_tail(ins))


def final_sum(*refs):
    *ins, out_ref, dg_ref = refs
    out_ref[...] = sum_rows(ins)
    dg_ref[...] = sum_tail(ins)


def first_input_grad(cot_ref, p_ref, dc_ref, w_ref, out_ref):
    input_grad(out_ref, cot_ref, p_ref[...].astype(BF16), dc_ref[...], w_ref)


def first_input_grad_out(cot_ref, p_ref, dc_ref, w_ref, out_ref, grad_ref, sems):
    stores = []

    def send(at, cols):
        stores.append(pltpu.make_async_copy(grad_ref.at[:, cols], out_ref.at[:, cols], sems.at[at]))
        stores[-1].start()

    input_grad(grad_ref, cot_ref, p_ref[...].astype(BF16), dc_ref[...], w_ref, send)
    for moved in stores:
        moved.wait()


def store(value_ref, out_ref):
    pltpu.sync_copy(value_ref, out_ref)


def kernel_call(body, args, outs, scratch=(), flops=0, from_hbm=0, out_space=pltpu.VMEM):
    local, far = pl.BlockSpec(memory_space=pltpu.VMEM), pl.BlockSpec(memory_space=pltpu.HBM)
    return pl.pallas_call(
        body,
        out_shape=outs,
        in_specs=[far] * from_hbm + [local] * (len(args) - from_hbm),
        out_specs=[pl.BlockSpec(memory_space=out_space)] * len(outs),
        scratch_shapes=scratch,
        compiler_params=pltpu.CompilerParams(vmem_limit_bytes=VMEM_LIMIT),
        name=getattr(body, "func", body).__name__,
        cost_estimate=pl.CostEstimate(flops=flops, bytes_accessed=4 << 20, transcendentals=0),
    )(*[pltpu.with_memory_space_constraint(v, pltpu.HBM) if i < from_hbm else v for i, v in enumerate(args)])


GATHER = (
    ("Y0", "y", "O0", ()),
    ("O1", "z", "O0", ()),
    ("O3", "r", "O0", ()),
    ("X0", "x", "O0", ()),
    ("D0", "x", "Y0", ("G", "H")),
    ("Y1", "y", "O1", ("Y0",)),
    ("X1", "x", "O1", ("Y0",)),
    ("O2", "r", "O3", ("X0", "O1", "Y0")),
    ("Y3", "y", "O3", ("X0", "O1", "Y0")),
    ("D3", "r", "D0", ("Y1", "O3", "X0")),
    ("X3", "x", "O3", ("D0", "Y1", "X0")),
    ("Y2", "y", "O2", ("D0", "Y1", "O3")),
    ("D1", "y", "X1", ("Y3", "O2", "D0")),
    ("X2", "x", "O2", ("Y3", "X1", "D0")),
    ("D2", "r", "D3", ("Y3", "X1", "O2")),
)
SCATTER = (
    ("D2", "z", "D1", ()),
    ("Y2", "y", "O2", ()),
    ("D3", "x", "Y3", ()),
    ("R", "", "", ()),
    ("Y1", "y", "O1", ()),
    ("X2", "x", "O2", ()),
    ("D1", "z", "D0", ()),
    ("Y3", "y", "O3", ("D2",)),
    ("X3", "x", "O3", ("D3", "Y2", "D2")),
    ("O2", "z", "O1", ("R", "D3", "D2")),
    ("D0", "y", "X0", ("Y1", "R", "D3")),
    ("X1", "x", "O1", ("X2", "Y1", "R")),
    ("F", "", "", ("D1", "X2", "Y1")),
    ("O3", "r", "O0", ("D1", "X2", "Y1")),
    ("Y0", "y", "O0", ("Y3", "D1", "X2")),
    ("X0", "x", "O0", ("F", "X3", "Y3")),
    ("O1", "z", "O0", ("F", "X3", "Y3")),
)
FIRST_AFTER = ("Y2", "X3")
PLACES = tuple(tuple(column + str(k) for column in columns for k in range(4)) for columns in ("OY", "XD"))
BACK = {"x": "x", "y": "y", "z": "r", "r": "z"}


def moves_between():
    def pairs(change):
        found = []
        for i in range(32):
            s, d = divmod(i, 8)
            to_s, to_d = change(s, d)
            found.append((i, to_s * 8 + to_d))
        return found

    following = {0: 1, 1: 3, 3: 2, 2: 0}
    last = {after: before for before, after in following.items()}
    changes = {
        "core": lambda s, d: (s ^ 1, d),
        "x": lambda s, d: (s ^ 2, d),
        "y": lambda s, d: (s, d ^ 1),
        "z": lambda s, d: (s, following[d >> 1] * 2 + (d & 1)),
        "r": lambda s, d: (s, last[d >> 1] * 2 + (d & 1)),
    }
    return {name: functools.partial(lambda v, p: lax.ppermute(v, AXES, p), p=pairs(c)) for name, c in changes.items()}


def after(value, others):
    return lax.optimization_barrier((value, *others))[0] if others else value


def gather(held, moves):
    for place, way, source, earlier in GATHER:
        held[place] = moves[way](after(held[source], [held[name] for name in earlier]))


def scatter(parts, beside, moves):
    rows, latent = parts["O0"].shape
    piece = jax.ShapeDtypeStruct((rows, latent), BF16)
    sums = [jax.ShapeDtypeStruct((rows - TAIL, latent), F32), jax.ShapeDtypeStruct((1, latent), F32)]
    into, held = {}, {}
    for place, _, source, _ in SCATTER:
        into.setdefault(source, []).append(place)
    for place, way, _, earlier in SCATTER:
        earlier = [held[name] for name in earlier]
        if place in beside:
            held[place] = beside[place](earlier)
            continue
        value = parts[place]
        if place in into:
            value = kernel_call(partial_sum, (value, *[held[name] for name in into[place]]), [piece])[0]
        held[place] = moves[BACK[way]](after(value, earlier))
    sums = kernel_call(final_sum, (parts["O0"], *[held[name] for name in into["O0"]]), sums)
    return sums, held


def on_chip_relay(h_forward, h_reverse, weights, gains):
    moves = moves_between()
    other_core = moves["core"]
    tokens, width = h_forward.shape[2:]
    rows, latent = weights.shape[1:]
    x_fwd, x_rev = h_forward[0, 0], other_core(h_reverse[0, 0])
    both_gains = jnp.concatenate([gains, moves["x"](gains)], axis=0)
    held = {"O0": weights[0], "G": both_gains, "H": x_rev}
    gather(held, moves)

    one = jax.ShapeDtypeStruct((tokens, width), BF16)
    matrix = jax.ShapeDtypeStruct((width, latent), BF16)
    saved_c = jax.ShapeDtypeStruct((tokens, latent), F32)
    saved_p = jax.ShapeDtypeStruct((tokens, tokens), F32)
    dgains = jax.ShapeDtypeStruct((1, latent), F32)
    dcs = jax.ShapeDtypeStruct((tokens, latent), BF16)
    piece = jax.ShapeDtypeStruct((rows + TAIL, latent), BF16)
    product = 2 * tokens * width * latent

    x1, x2, w, c1, p1 = (x_fwd, x_rev), [None] * 2, [None] * 2, [None] * 2, [None] * 2
    first = [one, matrix, saved_c, saved_p]
    chunks = pltpu.SemaphoreType.DMA((width // CHUNK + 1,))
    gain = after(both_gains, [held[name] for name in FIRST_AFTER])
    own, *others = [held[name] for name in PLACES[0]]
    u, w[0], c1[0], p1[0] = kernel_call(
        first_block_own, (own, x_fwd, *others, gain), first, [pltpu.VMEM((tokens, width), BF16), chunks], 2 * product, from_hbm=2
    )
    x2[0] = other_core(u)
    gain = after(both_gains, [c1[0]])
    u, w[1], c1[1], p1[1] = kernel_call(first_block_other, (*[held[name] for name in PLACES[1]], gain, x_rev), first, flops=2 * product)
    x2[1] = other_core(u)
    cot, dc2, dg2 = [None] * 2, [None] * 2, [None] * 2
    for chain in range(2):
        gain = after(both_gains, [dc2[0]] if chain else [])
        e, dc2[chain], dg2[chain] = kernel_call(
            functools.partial(second_block, chain), (gain, x2[chain], *w), [one, dcs, dgains],
            [pltpu.VMEM((tokens, width), BF16), pltpu.VMEM((tokens, latent), F32)], 4 * product,
        )
        cot[chain] = other_core(e)
    parts, dc1 = [None] * 2, [None] * 2
    for slot in range(2):
        dc1[slot], *parts[slot] = kernel_call(
            functools.partial(first_weight_grad, slot),
            (both_gains, x1[slot], c1[slot], p1[slot], cot[slot], *x2, *dc2, *dg2), [dcs] + [piece] * 8,
            [pltpu.VMEM((width, latent), BF16), pltpu.VMEM((2 * tokens, latent), BF16), pltpu.VMEM((1, latent), F32)],
            4 * product,
        )

    def input_grads(slot, earlier):
        args = (after(cot[slot], earlier), p1[slot], dc1[slot], w[slot])
        if slot == 0:
            scratch = [pltpu.VMEM((tokens, width), BF16), chunks]
            return kernel_call(first_input_grad_out, args, [one], scratch, 2 * product, out_space=pltpu.HBM)[0]
        (grad,) = kernel_call(first_input_grad, args, [one], flops=2 * product)
        return kernel_call(store, (other_core(grad),), [one], out_space=pltpu.HBM)[0]

    beside = {"F": functools.partial(input_grads, 0), "R": functools.partial(input_grads, 1)}
    parts = {name: part for slot in range(2) for name, part in zip(PLACES[slot], parts[slot])}
    (grad_weights, dgain), held = scatter(parts, beside, moves)
    return held["F"][None, None], held["R"][None, None], grad_weights[None], dgain


def from_partner(value, axis, apart):
    mask = 2**apart
    pairs = [(source, source ^ mask) for source in range(lax.axis_size(axis))]
    return lax.ppermute(value, axis, pairs)


def passed_along(value, axis, by):
    devices = lax.axis_size(axis)
    return lax.ppermute(value, axis, [(i, (i + by) % devices) for i in range(devices)])


def group_forward(x, w, g):
    c = jnp.dot(x, w, preferred_element_type=jnp.float32)
    inv = lax.rsqrt(jnp.mean(c * c, axis=-1, keepdims=True) + EPS)
    normed = (c * inv * g.astype(jnp.float32)).astype(jnp.bfloat16)
    scale = 3.0 / c.shape[-1]
    scores = jnp.dot(normed, normed.T, preferred_element_type=jnp.float32) * scale
    count = x.shape[0]
    rows = lax.broadcasted_iota(jnp.int32, (count, count), 0)
    cols = lax.broadcasted_iota(jnp.int32, (count, count), 1)
    scores = jnp.where(cols <= rows, scores, -1e30)
    top = jnp.max(scores, axis=-1, keepdims=True)
    expo = jnp.exp(scores - top)
    probs = expo / jnp.sum(expo, axis=-1, keepdims=True)
    probs_b = probs.astype(jnp.bfloat16)
    mixed = jnp.dot(probs_b, x, preferred_element_type=jnp.float32)
    out = (x.astype(jnp.float32) + mixed).astype(jnp.bfloat16)
    return (out, (c, inv, normed, probs, probs_b))


def group_backward(x, w, g, saved, grad_out):
    c, inv, normed, probs, probs_b = saved
    scale = 3.0 / c.shape[-1]
    dx = grad_out.astype(jnp.float32) + jnp.dot(
        probs_b.T, grad_out, preferred_element_type=jnp.float32
    )
    dprobs = jnp.dot(grad_out, x.T, preferred_element_type=jnp.float32)
    dscores = probs * (dprobs - jnp.sum(dprobs * probs, axis=-1, keepdims=True))
    dscores_b = (dscores * scale).astype(jnp.bfloat16)
    dnormed = jnp.dot(dscores_b, normed, preferred_element_type=jnp.float32) + jnp.dot(
        dscores_b.T, normed, preferred_element_type=jnp.float32
    )
    dgain = jnp.sum(dnormed * c * inv, axis=0)
    dhat = dnormed * g.astype(jnp.float32)
    dc = inv * dhat - c * (inv * inv * inv) * jnp.mean(dhat * c, axis=-1, keepdims=True)
    dc_b = dc.astype(jnp.bfloat16)
    dx = dx + jnp.dot(dc_b, w.T, preferred_element_type=jnp.float32)
    dw = jnp.dot(x.T, dc_b, preferred_element_type=jnp.float32)
    return (dx, dw, dgain)


def twin_copy(pair):
    for bit in range(lax.axis_size("section").bit_length() - 1):
        pair = from_partner((pair[0], pair[1]), "section", bit)
    return (pair[0], pair[1])


def grad_twin(pair):
    for bit in range(lax.axis_size("section").bit_length() - 1):
        pair = (
            from_partner(pair[0].astype(jnp.bfloat16), "section", bit).astype(jnp.float32),
            from_partner(pair[1].astype(jnp.bfloat16), "section", bit).astype(jnp.float32),
        )
    return (pair[0], pair[1])


def neighbour(values, offset):
    return passed_along(values, "section", offset)


def sections_apart(h_forward, h_reverse, weights, gains):
    shard = weights[0]
    gain = gains[0]
    twin_shard, twin_gain = twin_copy((shard, gain))
    own, twin = (
        lax.all_gather(shard, "dp", axis=0, tiled=True),
        lax.all_gather(twin_shard, "dp", axis=0, tiled=True),
    )
    x_fwd = h_forward[0, 0]
    x_rev = h_reverse[0, 0]
    u_fwd, saved_f1 = group_forward(x_fwd, own, gain)
    u_rev, saved_r1 = group_forward(x_rev, twin, twin_gain)
    in_fwd = neighbour(u_fwd, 1)
    in_rev = neighbour(u_rev, -1)
    v_fwd, saved_f2 = group_forward(in_fwd, own, gain)
    v_rev, saved_r2 = group_forward(in_rev, twin, twin_gain)
    din_fwd, dw_f2, dg_f2 = group_backward(in_fwd, own, gain, saved_f2, v_fwd)
    din_rev, dw_r2, dg_r2 = group_backward(in_rev, twin, twin_gain, saved_r2, v_rev)
    back_fwd = neighbour(din_fwd.astype(jnp.bfloat16), -1)
    back_rev = neighbour(din_rev.astype(jnp.bfloat16), 1)
    dh_fwd, dw_f1, dg_f1 = group_backward(x_fwd, own, gain, saved_f1, back_fwd)
    dh_rev, dw_r1, dg_r1 = group_backward(x_rev, twin, twin_gain, saved_r1, back_rev)
    share_fwd, share_rev = (
        lax.psum_scatter(
            (dw_f1 + dw_f2).astype(jnp.bfloat16), "dp", scatter_dimension=0, tiled=True
        ).astype(jnp.float32),
        lax.psum_scatter(
            (dw_r1 + dw_r2).astype(jnp.bfloat16), "dp", scatter_dimension=0, tiled=True
        ).astype(jnp.float32),
    )
    gsum_fwd, gsum_rev = lax.psum((dg_f1 + dg_f2, dg_r1 + dg_r2), "dp")
    mirror_w, mirror_g = grad_twin((share_rev, gsum_rev))
    grad_weights = (share_fwd + mirror_w)[None]
    grad_gains = (gsum_fwd + mirror_g)[None]
    return (
        dh_fwd.astype(jnp.bfloat16)[None, None],
        dh_rev.astype(jnp.bfloat16)[None, None],
        grad_weights,
        grad_gains,
    )


def solution(mesh):
    in_specs = (
        P("section", "dp", None, None),
        P("section", "dp", None, None),
        P("section", "dp", None),
        P("section", None),
    )
    out_specs = (
        P("section", "dp", None, None),
        P("section", "dp", None, None),
        P("section", "dp", None),
        P("section", None),
    )
    on_chip = (mesh.shape["section"], mesh.shape["dp"]) == (4, 8)
    on_device = on_chip_relay if on_chip else sections_apart
    return jax.shard_map(
        on_device, mesh=mesh, in_specs=in_specs, out_specs=out_specs, check_vma=False
    )
```

```python
import functools

import jax
import jax.numpy as jnp
from jax import lax
from jax.experimental import pallas as pl
from jax.experimental.pallas import tpu as pltpu
from jax.sharding import PartitionSpec as P

EPS = 1e-06
AXES = ("section", "dp")
BF16 = jnp.bfloat16
F32 = jnp.float32
CHUNK = 512
TAIL = 16
VMEM_LIMIT = 40 * 1024 * 1024


def matmul(a, b):
    return jnp.dot(a, b, preferred_element_type=F32)


def matmul_nt(a, b):
    return lax.dot_general(a, b, (((1,), (1,)), ((), ())), preferred_element_type=F32)


def matmul_tn(a, b):
    return lax.dot_general(a, b, (((0,), (0,)), ((), ())), preferred_element_type=F32)


def latent_norm(c, g):
    inv = lax.rsqrt(jnp.mean(c * c, axis=-1, keepdims=True) + EPS)
    return inv, (c * inv * g.astype(F32)).astype(BF16)


def attention(normed, width):
    scores = matmul_nt(normed, normed) * (3.0 / width)
    rows = lax.broadcasted_iota(jnp.int32, scores.shape, 0)
    cols = lax.broadcasted_iota(jnp.int32, scores.shape, 1)
    scores = jnp.where(cols <= rows, scores, -1e30)
    expo = jnp.exp(scores - jnp.max(scores, axis=-1, keepdims=True))
    return expo / jnp.sum(expo, axis=-1, keepdims=True)


def column_chunks(width):
    return [slice(at, at + CHUNK) for at in range(0, width, CHUNK)]


def mix_into(out_ref, x_ref, probs_b):
    for cols in column_chunks(x_ref.shape[-1]):
        x = x_ref[:, cols]
        out_ref[:, cols] = (x.astype(F32) + matmul(probs_b, x)).astype(BF16)


def score_grad(dy_ref, x_ref):
    total = None
    for cols in column_chunks(x_ref.shape[-1]):
        part = matmul_nt(dy_ref[:, cols], x_ref[:, cols])
        total = part if total is None else total + part
    return total


def latent_grad(dprobs, probs, c, inv, normed, g):
    scale = 3.0 / c.shape[-1]
    dscores = probs * (dprobs - jnp.sum(dprobs * probs, axis=-1, keepdims=True))
    dscores_b = (dscores * scale).astype(BF16)
    dnormed = matmul(dscores_b, normed) + matmul_tn(dscores_b, normed)
    dgain = jnp.sum(dnormed * c * inv, axis=0, keepdims=True)
    dhat = dnormed * g.astype(F32)
    dc = inv * dhat - c * (inv * inv * inv) * jnp.mean(dhat * c, axis=-1, keepdims=True)
    return dc.astype(BF16), dgain


def input_grad(out_ref, dy_ref, probs_b, dc_b, w_ref, after_chunk=None):
    left = jnp.concatenate([probs_b.astype(F32).T.astype(BF16), dc_b], axis=1)
    for at, cols in enumerate(column_chunks(dy_ref.shape[-1])):
        dy = dy_ref[:, cols]
        dx = dy.astype(F32) + matmul(left, jnp.concatenate([dy, w_ref[cols, :].T], axis=0))
        out_ref[:, cols] = dx.astype(BF16)
        if after_chunk is not None:
            after_chunk(at, cols)


def ring_place(value):
    return value ^ (value >> 1)


def shard_row(dy, steps, rows):
    dp = lax.axis_index("dp")
    place = (ring_place(dp >> 1) + steps) & 3
    return pl.multiple_of((ring_place(place) * 2 + ((dp & 1) ^ dy)) * rows, 16)


def slot_of(chain):
    return chain ^ 1 ^ (lax.axis_index("section") & 1)


def place_shards(w_ref, pieces):
    rows = pieces[-1].shape[0]
    for at, piece in enumerate(pieces):
        if piece is not None:
            w_ref[pl.ds(shard_row(at // 4, 4 - at % 4, rows), rows), :] = piece[...]


def first_output(slot, c, gain_ref, x_ref, u_ref, c_ref, p_ref):
    _, normed = latent_norm(c, gain_ref[slot : slot + 1, :])
    probs = attention(normed, c.shape[-1])
    c_ref[...] = c
    p_ref[...] = probs
    mix_into(u_ref, x_ref, probs.astype(BF16))


def first_block_own(own_ref, x_hbm_ref, *refs):
    pieces, (gain_ref, u_ref, w_ref, c_ref, p_ref, x_ref, sems) = refs[:7], refs[7:]
    rows = own_ref.shape[0]
    own = pltpu.make_async_copy(own_ref, w_ref.at[pl.ds(shard_row(0, 0, rows), rows), :], sems.at[0])
    chunks = column_chunks(x_ref.shape[-1])
    loads = [pltpu.make_async_copy(x_hbm_ref.at[:, cols], x_ref.at[:, cols], sems.at[1 + i]) for i, cols in enumerate(chunks)]
    for load in (own, *loads):
        load.start()
    place_shards(w_ref, (None, *pieces))
    own.wait()
    c = 0.0
    for load, cols in zip(loads, chunks):
        load.wait()
        c = c + matmul(x_ref[:, cols], w_ref[cols, :])
    first_output(0, c, gain_ref, x_ref, u_ref, c_ref, p_ref)


def first_block_other(*refs):
    pieces, (gain_ref, x_ref, u_ref, w_ref, c_ref, p_ref) = refs[:8], refs[8:]
    place_shards(w_ref, pieces)
    first_output(1, matmul(x_ref[...], w_ref[...]), gain_ref, x_ref, u_ref, c_ref, p_ref)


def second_block(chain, gain_ref, x_ref, w0_ref, w1_ref, e_ref, dc_ref, dg_ref, v_ref, c_ref):
    slot = slot_of(chain)
    g = jnp.where(slot == 0, gain_ref[0:1, :].astype(F32), gain_ref[1:2, :].astype(F32))
    for at, w_ref in enumerate((w0_ref, w1_ref)):

        @pl.when(slot == at)
        def _(w_ref=w_ref):
            c_ref[...] = matmul(x_ref[...], w_ref[...])

    c = c_ref[...]
    inv, normed = latent_norm(c, g)
    probs = attention(normed, c.shape[-1])
    probs_b = probs.astype(BF16)
    mix_into(v_ref, x_ref, probs_b)
    dc_b, dgain = latent_grad(score_grad(v_ref, x_ref), probs, c, inv, normed, g)
    dc_ref[...] = dc_b
    dg_ref[...] = dgain
    for at, w_ref in enumerate((w0_ref, w1_ref)):

        @pl.when(slot == at)
        def _(w_ref=w_ref):
            input_grad(e_ref, v_ref, probs_b, dc_b, w_ref)


def first_weight_grad(slot, *refs):
    gain_ref, x_ref, c_ref, p_ref, cot_ref, x2a_ref, x2b_ref, dc2a_ref, dc2b_ref, dg2a_ref, dg2b_ref = refs[:11]
    dc_ref, pieces, (dw_ref, dcs_ref, dg_ref) = refs[11], refs[12:20], refs[20:]
    tokens, rows = x_ref.shape[0], pieces[0].shape[0] - TAIL
    g = gain_ref[slot : slot + 1, :]
    c, probs = c_ref[...], p_ref[...]
    inv, normed = latent_norm(c, g)
    dc_b, dgain = latent_grad(score_grad(cot_ref, x_ref), probs, c, inv, normed, g)
    dc_ref[...] = dc_b
    dcs_ref[:tokens, :] = dc_b
    for chain, x2_ref, dc2_ref, dg2_ref in ((0, x2a_ref, dc2a_ref, dg2a_ref), (1, x2b_ref, dc2b_ref, dg2b_ref)):

        @pl.when(slot_of(chain) == slot)
        def _(x2_ref=x2_ref, dc2_ref=dc2_ref, dg2_ref=dg2_ref):
            dg_ref[...] = dgain + dg2_ref[...]
            dcs_ref[tokens:, :] = dc2_ref[...]
            for cols in column_chunks(x_ref.shape[-1]):
                x = jnp.concatenate([x_ref[:, cols], x2_ref[:, cols]], axis=0)
                dw_ref[cols, :] = matmul_tn(x, dcs_ref[...]).astype(BF16)

    tail = split_tail(dg_ref[...])
    for at, piece in enumerate(pieces):
        piece[:rows, :] = dw_ref[pl.ds(shard_row(at // 4, 4 - at % 4, rows), rows), :]
        piece[rows:, :] = tail


def split_tail(dgain):
    high = dgain.astype(BF16).astype(F32)
    at = lax.broadcasted_iota(jnp.int32, (TAIL, dgain.shape[-1]), 0)
    return jnp.where(at == 0, high, jnp.where(at == 1, dgain - high, 0.0)).astype(BF16)


def sum_rows(refs):
    return sum(ref[:-TAIL, :].astype(F32) for ref in refs)


def sum_tail(refs):
    tail = sum(ref[-TAIL:, :].astype(F32) for ref in refs)
    return tail[0:1, :] + tail[1:2, :]


def partial_sum(*refs):
    *ins, out_ref = refs
    out_ref[:-TAIL, :] = sum_rows(ins).astype(BF16)
    out_ref[-TAIL:, :] = split_tail(sum_tail(ins))


def final_sum(*refs):
    *ins, out_ref, dg_ref = refs
    out_ref[...] = sum_rows(ins)
    dg_ref[...] = sum_tail(ins)


def first_input_grad(cot_ref, p_ref, dc_ref, w_ref, out_ref):
    input_grad(out_ref, cot_ref, p_ref[...].astype(BF16), dc_ref[...], w_ref)


def first_input_grad_out(cot_ref, p_ref, dc_ref, w_ref, out_ref, grad_ref, sems):
    stores = []

    def send(at, cols):
        stores.append(pltpu.make_async_copy(grad_ref.at[:, cols], out_ref.at[:, cols], sems.at[at]))
        stores[-1].start()

    input_grad(grad_ref, cot_ref, p_ref[...].astype(BF16), dc_ref[...], w_ref, send)
    for moved in stores:
        moved.wait()


def store(value_ref, out_ref):
    pltpu.sync_copy(value_ref, out_ref)


def kernel_call(body, args, outs, scratch=(), flops=0, from_hbm=0, out_space=pltpu.VMEM):
    local, far = pl.BlockSpec(memory_space=pltpu.VMEM), pl.BlockSpec(memory_space=pltpu.HBM)
    return pl.pallas_call(
        body,
        out_shape=outs,
        in_specs=[far] * from_hbm + [local] * (len(args) - from_hbm),
        out_specs=[pl.BlockSpec(memory_space=out_space)] * len(outs),
        scratch_shapes=scratch,
        compiler_params=pltpu.CompilerParams(vmem_limit_bytes=VMEM_LIMIT),
        name=getattr(body, "func", body).__name__,
        cost_estimate=pl.CostEstimate(flops=flops, bytes_accessed=4 << 20, transcendentals=0),
    )(*[pltpu.with_memory_space_constraint(v, pltpu.HBM) if i < from_hbm else v for i, v in enumerate(args)])


GATHER = (
    ("Y0", "y", "O0", ()),
    ("O1", "z", "O0", ()),
    ("O3", "r", "O0", ()),
    ("X0", "x", "O0", ()),
    ("D0", "x", "Y0", ("G", "H")),
    ("Y1", "y", "O1", ()),
    ("X1", "x", "O1", ("Y0",)),
    ("O2", "r", "O3", ("X0", "O1", "Y0")),
    ("Y3", "y", "O3", ("X0", "O1", "Y0")),
    ("D3", "r", "D0", ("Y1", "O3", "X0")),
    ("D1", "y", "X1", ("Y3", "O2", "D0")),
    ("X3", "x", "O3", ()),
    ("Y2", "y", "O2", ("D0", "Y1", "O3")),
    ("X2", "x", "O2", ("Y3", "X1", "D0")),
    ("D2", "r", "D3", ("Y3", "X1", "O2")),
)
SCATTER = (
    ("D2", "z", "D1", ()),
    ("Y2", "y", "O2", ()),
    ("D3", "x", "Y3", ()),
    ("R", "", "", ()),
    ("Y1", "y", "O1", ()),
    ("X2", "x", "O2", ()),
    ("D1", "z", "D0", ()),
    ("Y3", "y", "O3", ("D2",)),
    ("X3", "x", "O3", ("D3", "Y2", "D2")),
    ("O2", "z", "O1", ("R", "D3", "D2")),
    ("D0", "y", "X0", ("Y1", "R", "D3")),
    ("X1", "x", "O1", ("X2", "Y1", "R")),
    ("F", "", "", ("D1", "X2", "Y1")),
    ("O3", "r", "O0", ("D1", "X2", "Y1")),
    ("Y0", "y", "O0", ("Y3", "D1", "X2")),
    ("X0", "x", "O0", ("F", "X3", "Y3")),
    ("O1", "z", "O0", ("F", "X3", "Y3")),
)
FIRST_AFTER = ("Y2", "X3")
PLACES = tuple(tuple(column + str(k) for column in columns for k in range(4)) for columns in ("OY", "XD"))
BACK = {"x": "x", "y": "y", "z": "r", "r": "z"}


def moves_between():
    def pairs(change):
        found = []
        for i in range(32):
            s, d = divmod(i, 8)
            to_s, to_d = change(s, d)
            found.append((i, to_s * 8 + to_d))
        return found

    following = {0: 1, 1: 3, 3: 2, 2: 0}
    last = {after: before for before, after in following.items()}
    changes = {
        "core": lambda s, d: (s ^ 1, d),
        "x": lambda s, d: (s ^ 2, d),
        "y": lambda s, d: (s, d ^ 1),
        "z": lambda s, d: (s, following[d >> 1] * 2 + (d & 1)),
        "r": lambda s, d: (s, last[d >> 1] * 2 + (d & 1)),
    }
    return {name: functools.partial(lambda v, p: lax.ppermute(v, AXES, p), p=pairs(c)) for name, c in changes.items()}


def after(value, others):
    return lax.optimization_barrier((value, *others))[0] if others else value


def gather(held, moves):
    for place, way, source, earlier in GATHER:
        held[place] = moves[way](after(held[source], [held[name] for name in earlier]))


def scatter(parts, beside, moves):
    rows, latent = parts["O0"].shape
    piece = jax.ShapeDtypeStruct((rows, latent), BF16)
    sums = [jax.ShapeDtypeStruct((rows - TAIL, latent), F32), jax.ShapeDtypeStruct((1, latent), F32)]
    into, held = {}, {}
    for place, _, source, _ in SCATTER:
        into.setdefault(source, []).append(place)
    for place, way, _, earlier in SCATTER:
        earlier = [held[name] for name in earlier]
        if place in beside:
            held[place] = beside[place](earlier)
            continue
        value = parts[place]
        if place in into:
            value = kernel_call(partial_sum, (value, *[held[name] for name in into[place]]), [piece])[0]
        held[place] = moves[BACK[way]](after(value, earlier))
    sums = kernel_call(final_sum, (parts["O0"], *[held[name] for name in into["O0"]]), sums)
    return sums, held


def on_chip_relay(h_forward, h_reverse, weights, gains):
    moves = moves_between()
    other_core = moves["core"]
    tokens, width = h_forward.shape[2:]
    rows, latent = weights.shape[1:]
    x_fwd, x_rev = h_forward[0, 0], other_core(h_reverse[0, 0])
    both_gains = jnp.concatenate([gains, moves["x"](gains)], axis=0)
    held = {"O0": weights[0], "G": both_gains, "H": x_rev}
    gather(held, moves)

    one = jax.ShapeDtypeStruct((tokens, width), BF16)
    matrix = jax.ShapeDtypeStruct((width, latent), BF16)
    saved_c = jax.ShapeDtypeStruct((tokens, latent), F32)
    saved_p = jax.ShapeDtypeStruct((tokens, tokens), F32)
    dgains = jax.ShapeDtypeStruct((1, latent), F32)
    dcs = jax.ShapeDtypeStruct((tokens, latent), BF16)
    piece = jax.ShapeDtypeStruct((rows + TAIL, latent), BF16)
    product = 2 * tokens * width * latent

    x1, x2, w, c1, p1 = (x_fwd, x_rev), [None] * 2, [None] * 2, [None] * 2, [None] * 2
    first = [one, matrix, saved_c, saved_p]
    chunks = pltpu.SemaphoreType.DMA((width // CHUNK + 1,))
    gain = after(both_gains, [held[name] for name in FIRST_AFTER])
    own, *others = [held[name] for name in PLACES[0]]
    u, w[0], c1[0], p1[0] = kernel_call(
        first_block_own, (own, x_fwd, *others, gain), first, [pltpu.VMEM((tokens, width), BF16), chunks], 2 * product, from_hbm=2
    )
    x2[0] = other_core(u)
    gain = after(both_gains, [c1[0]])
    u, w[1], c1[1], p1[1] = kernel_call(first_block_other, (*[held[name] for name in PLACES[1]], gain, x_rev), first, flops=2 * product)
    x2[1] = other_core(u)
    cot, dc2, dg2 = [None] * 2, [None] * 2, [None] * 2
    for chain in range(2):
        gain = after(both_gains, [dc2[0]] if chain else [])
        e, dc2[chain], dg2[chain] = kernel_call(
            functools.partial(second_block, chain), (gain, x2[chain], *w), [one, dcs, dgains],
            [pltpu.VMEM((tokens, width), BF16), pltpu.VMEM((tokens, latent), F32)], 4 * product,
        )
        cot[chain] = other_core(e)
    parts, dc1 = [None] * 2, [None] * 2
    for slot in range(2):
        dc1[slot], *parts[slot] = kernel_call(
            functools.partial(first_weight_grad, slot),
            (both_gains, x1[slot], c1[slot], p1[slot], cot[slot], *x2, *dc2, *dg2), [dcs] + [piece] * 8,
            [pltpu.VMEM((width, latent), BF16), pltpu.VMEM((2 * tokens, latent), BF16), pltpu.VMEM((1, latent), F32)],
            4 * product,
        )

    def input_grads(slot, earlier):
        args = (after(cot[slot], earlier), p1[slot], dc1[slot], w[slot])
        if slot == 0:
            scratch = [pltpu.VMEM((tokens, width), BF16), chunks]
            return kernel_call(first_input_grad_out, args, [one], scratch, 2 * product, out_space=pltpu.HBM)[0]
        (grad,) = kernel_call(first_input_grad, args, [one], flops=2 * product)
        return kernel_call(store, (other_core(grad),), [one], out_space=pltpu.HBM)[0]

    beside = {"F": functools.partial(input_grads, 0), "R": functools.partial(input_grads, 1)}
    parts = {name: part for slot in range(2) for name, part in zip(PLACES[slot], parts[slot])}
    (grad_weights, dgain), held = scatter(parts, beside, moves)
    return held["F"][None, None], held["R"][None, None], grad_weights[None], dgain


def from_partner(value, axis, apart):
    mask = 2**apart
    pairs = [(source, source ^ mask) for source in range(lax.axis_size(axis))]
    return lax.ppermute(value, axis, pairs)


def passed_along(value, axis, by):
    devices = lax.axis_size(axis)
    return lax.ppermute(value, axis, [(i, (i + by) % devices) for i in range(devices)])


def group_forward(x, w, g):
    c = jnp.dot(x, w, preferred_element_type=jnp.float32)
    inv = lax.rsqrt(jnp.mean(c * c, axis=-1, keepdims=True) + EPS)
    normed = (c * inv * g.astype(jnp.float32)).astype(jnp.bfloat16)
    scale = 3.0 / c.shape[-1]
    scores = jnp.dot(normed, normed.T, preferred_element_type=jnp.float32) * scale
    count = x.shape[0]
    rows = lax.broadcasted_iota(jnp.int32, (count, count), 0)
    cols = lax.broadcasted_iota(jnp.int32, (count, count), 1)
    scores = jnp.where(cols <= rows, scores, -1e30)
    top = jnp.max(scores, axis=-1, keepdims=True)
    expo = jnp.exp(scores - top)
    probs = expo / jnp.sum(expo, axis=-1, keepdims=True)
    probs_b = probs.astype(jnp.bfloat16)
    mixed = jnp.dot(probs_b, x, preferred_element_type=jnp.float32)
    out = (x.astype(jnp.float32) + mixed).astype(jnp.bfloat16)
    return (out, (c, inv, normed, probs, probs_b))


def group_backward(x, w, g, saved, grad_out):
    c, inv, normed, probs, probs_b = saved
    scale = 3.0 / c.shape[-1]
    dx = grad_out.astype(jnp.float32) + jnp.dot(
        probs_b.T, grad_out, preferred_element_type=jnp.float32
    )
    dprobs = jnp.dot(grad_out, x.T, preferred_element_type=jnp.float32)
    dscores = probs * (dprobs - jnp.sum(dprobs * probs, axis=-1, keepdims=True))
    dscores_b = (dscores * scale).astype(jnp.bfloat16)
    dnormed = jnp.dot(dscores_b, normed, preferred_element_type=jnp.float32) + jnp.dot(
        dscores_b.T, normed, preferred_element_type=jnp.float32
    )
    dgain = jnp.sum(dnormed * c * inv, axis=0)
    dhat = dnormed * g.astype(jnp.float32)
    dc = inv * dhat - c * (inv * inv * inv) * jnp.mean(dhat * c, axis=-1, keepdims=True)
    dc_b = dc.astype(jnp.bfloat16)
    dx = dx + jnp.dot(dc_b, w.T, preferred_element_type=jnp.float32)
    dw = jnp.dot(x.T, dc_b, preferred_element_type=jnp.float32)
    return (dx, dw, dgain)


def twin_copy(pair):
    for bit in range(lax.axis_size("section").bit_length() - 1):
        pair = from_partner((pair[0], pair[1]), "section", bit)
    return (pair[0], pair[1])


def grad_twin(pair):
    for bit in range(lax.axis_size("section").bit_length() - 1):
        pair = (
            from_partner(pair[0].astype(jnp.bfloat16), "section", bit).astype(jnp.float32),
            from_partner(pair[1].astype(jnp.bfloat16), "section", bit).astype(jnp.float32),
        )
    return (pair[0], pair[1])


def neighbour(values, offset):
    return passed_along(values, "section", offset)


def sections_apart(h_forward, h_reverse, weights, gains):
    shard = weights[0]
    gain = gains[0]
    twin_shard, twin_gain = twin_copy((shard, gain))
    own, twin = (
        lax.all_gather(shard, "dp", axis=0, tiled=True),
        lax.all_gather(twin_shard, "dp", axis=0, tiled=True),
    )
    x_fwd = h_forward[0, 0]
    x_rev = h_reverse[0, 0]
    u_fwd, saved_f1 = group_forward(x_fwd, own, gain)
    u_rev, saved_r1 = group_forward(x_rev, twin, twin_gain)
    in_fwd = neighbour(u_fwd, 1)
    in_rev = neighbour(u_rev, -1)
    v_fwd, saved_f2 = group_forward(in_fwd, own, gain)
    v_rev, saved_r2 = group_forward(in_rev, twin, twin_gain)
    din_fwd, dw_f2, dg_f2 = group_backward(in_fwd, own, gain, saved_f2, v_fwd)
    din_rev, dw_r2, dg_r2 = group_backward(in_rev, twin, twin_gain, saved_r2, v_rev)
    back_fwd = neighbour(din_fwd.astype(jnp.bfloat16), -1)
    back_rev = neighbour(din_rev.astype(jnp.bfloat16), 1)
    dh_fwd, dw_f1, dg_f1 = group_backward(x_fwd, own, gain, saved_f1, back_fwd)
    dh_rev, dw_r1, dg_r1 = group_backward(x_rev, twin, twin_gain, saved_r1, back_rev)
    share_fwd, share_rev = (
        lax.psum_scatter(
            (dw_f1 + dw_f2).astype(jnp.bfloat16), "dp", scatter_dimension=0, tiled=True
        ).astype(jnp.float32),
        lax.psum_scatter(
            (dw_r1 + dw_r2).astype(jnp.bfloat16), "dp", scatter_dimension=0, tiled=True
        ).astype(jnp.float32),
    )
    gsum_fwd, gsum_rev = lax.psum((dg_f1 + dg_f2, dg_r1 + dg_r2), "dp")
    mirror_w, mirror_g = grad_twin((share_rev, gsum_rev))
    grad_weights = (share_fwd + mirror_w)[None]
    grad_gains = (gsum_fwd + mirror_g)[None]
    return (
        dh_fwd.astype(jnp.bfloat16)[None, None],
        dh_rev.astype(jnp.bfloat16)[None, None],
        grad_weights,
        grad_gains,
    )


def solution(mesh):
    in_specs = (
        P("section", "dp", None, None),
        P("section", "dp", None, None),
        P("section", "dp", None),
        P("section", None),
    )
    out_specs = (
        P("section", "dp", None, None),
        P("section", "dp", None, None),
        P("section", "dp", None),
        P("section", None),
    )
    on_chip = (mesh.shape["section"], mesh.shape["dp"]) == (4, 8)
    on_device = on_chip_relay if on_chip else sections_apart
    return jax.shard_map(
        on_device, mesh=mesh, in_specs=in_specs, out_specs=out_specs, check_vma=False
    )
```
